128 devices in a mesh: panel: 16 (over y_hi, x, core), snp: 8 (over z, y_lo).
Axes of the slice: x: 4, y: 4 (y_hi: 2, y_lo: 2; y = y_hi * 2 + y_lo), z: 4, core: 2. Of those that a mesh axis runs over, the one named last changes fastest.
Arguments:
- dosage: bfloat16 [32768, 8192], P('panel', 'snp'), may hold values from 0 to 2
- allele_freq: float32 [8192], P('snp'), may hold values from 0.05 to 0.5
- plan: int32 [2, 16], replicated, may hold values from 0 to 15, as said below
Outputs:
- relation: float32 [2, 32768, 2048], P(None, ('panel', 'snp'))
The draws below stay inside these ranges and needn't reach their ends.
Inputs may be any that keep to these rules, and one draw needn't show every extreme that they name: `plan`: each row pairs the 16 panels into 8 disjoint pairs: no panel meets itself, the partner of a panel's partner is that panel, and no pair meets in two rounds.
All inputs are finite; a program needn't handle non-finite values.
Results may differ from the reference program's by a relative error of at most 0.015.
Values may be sent and summed in bfloat16 or wider, within the bound.
A program may use at most 128 MiB of HBM per device.

```python
import math
import jax
import jax.numpy as jnp
from jax import lax

PANEL_ROWS = 2048
SNP_DEV = 1024
ROUNDS = 2
INDIV = 32768
M_TOTAL = 8192
N_PANEL = 16
N_SNP = 8


def frequency_table(key):
    freq_key = jax.random.fold_in(key, 101)
    uniform_part = jax.random.uniform(freq_key, (M_TOTAL,), jnp.float32)
    return 0.05 * jnp.power(10.0, uniform_part)


def draw_allele_freq(key, part):
    return frequency_table(key).astype(jnp.float32)


def draw_dosage(key, part):
    freq = frequency_table(key)
    key = jax.random.fold_in(key, 5)
    local_key = jax.random.fold_in(key, 0)
    offset = jax.random.uniform(local_key, (INDIV, M_TOTAL), jnp.float32, -1.0, 1.0)
    return (2.0 * freq * (1.0 + offset)).astype(jnp.bfloat16)


def draw_plan(key, part):
    key = jax.random.fold_in(key, 11)
    label_key, round_key = jax.random.split(key)
    labels = jax.random.permutation(label_key, N_PANEL).astype(jnp.int32)
    picked = jax.random.permutation(round_key, N_PANEL - 1)[:ROUNDS].astype(jnp.int32)
    modulus = N_PANEL - 1
    teams = jnp.arange(N_PANEL, dtype=jnp.int32)
    circle = jnp.mod(2 * picked[:, None] - teams[None, :], modulus)
    circle = jnp.where(circle == teams[None, :], N_PANEL - 1, circle)
    base = jnp.where(teams[None, :] == N_PANEL - 1, picked[:, None], circle)
    inverse = jnp.argsort(labels, stable=True).astype(jnp.int32)
    renamed = jnp.take(base, inverse, axis=1)
    return jnp.take(labels, renamed).astype(jnp.int32)


def setup_inputs(seed: int = 0) -> dict:
    seeds = jax.random.split(jax.random.key(seed), 4)
    return {
        "dosage": draw_dosage(jax.random.fold_in(seeds[3], 71), 0),
        "allele_freq": draw_allele_freq(jax.random.fold_in(seeds[3], 71), 0),
        "plan": draw_plan(jax.random.fold_in(seeds[3], 71), 0),
    }


def reference(dosage, allele_freq, plan):
    deviation = jnp.sqrt(2.0 * allele_freq * (1.0 - allele_freq))
    standard = ((dosage.astype(jnp.float32) - 2.0 * allele_freq) / deviation).astype(jnp.bfloat16)
    panels = standard.reshape(N_PANEL, PANEL_ROWS, N_SNP, SNP_DEV)
    scaling_multiplier = 1.0 / math.sqrt(M_TOTAL)

    def one_tile(position):
        which_round = position // N_PANEL
        member = position % N_PANEL
        partner = plan[which_round, member]
        local_block = panels[member].astype(jnp.float32)
        partner_block = panels[partner].astype(jnp.float32)
        partial_tile_value = jnp.einsum('tmr,vmr->mtv', local_block, partner_block) * scaling_multiplier
        partial_tile_value = lax.optimization_barrier(partial_tile_value.astype(jnp.bfloat16)).astype(jnp.float32)
        return lax.optimization_barrier(jnp.sum(partial_tile_value, axis=0))
    tiles = lax.map(one_tile, jnp.arange(ROUNDS * N_PANEL, dtype=jnp.int32))
    return tiles.reshape(ROUNDS, N_PANEL * PANEL_ROWS, PANEL_ROWS)
```

```python
import functools
import math

import jax
import jax.numpy as jnp
from jax import lax
from jax.experimental import pallas as pl
from jax.experimental.pallas import tpu as pltpu
from jax.sharding import PartitionSpec as P

MESH = pl.DeviceIdType.MESH
HALF = 8
ORDER = (2, 6, 4, 3, 7, 5, 1)


def wait_for(ref, sem):
    pltpu.make_async_copy(ref, ref, sem).wait()


def tables(plan_ref, step_ref, low_ref, colour_ref, to_ref, from_ref, rank_ref, n):
    def start(v, carry):
        nxt = plan_ref[1, plan_ref[0, v]]
        step_ref[0, v] = nxt
        low_ref[0, v] = jnp.minimum(v, nxt)
        return carry

    lax.fori_loop(0, n, start, 0)
    for j in range(2):

        def double(v, carry, j=j):
            nxt = step_ref[j, step_ref[j, v]]
            step_ref[j + 1, v] = nxt
            low_ref[j + 1, v] = jnp.minimum(low_ref[j, v], low_ref[j, nxt])
            return carry

        lax.fori_loop(0, n, double, 0)

    def settle(v, carry):
        first, second = plan_ref[0, v], plan_ref[1, v]
        zero = low_ref[2, v] < low_ref[2, first]
        colour_ref[v] = jnp.where(zero, 0, 1)
        from_ref[v] = jnp.where(zero, first, second)
        to_ref[v] = jnp.where(zero, second, first)
        return carry

    lax.fori_loop(0, n, settle, 0)

    def ranks(v, carry):
        a, b = carry
        restart = lax.rem(v, HALF) == 0
        a, b = jnp.where(restart, 0, a), jnp.where(restart, 0, b)
        rank_ref[0, v] = a
        rank_ref[1, v] = b
        mine = lax.div(v, HALF)
        a = a + jnp.where(lax.div(to_ref[v], HALF) != mine, 1, 0)
        b = b + jnp.where(lax.div(from_ref[v], HALF) != mine, 1, 0)
        return a, b

    lax.fori_loop(0, n, ranks, (jnp.int32(0), jnp.int32(0)))


def kernel(
    chunks, crossing, plan_ref, freq_ref, dosage_ref, own_ref, other_ref,
    std, pool, cross_out, arr_out, partner, part, zin, yout, yin, total,
    tout, tpool, tcross_out, tarr_out, tin, held, theld,
    step_ref, low_ref, colour_ref, to_ref, from_ref, rank_ref, slot_ref,
    load_sem, ssem, rsem,
):
    rows = 256 // chunks
    panel, snp = lax.axis_index("panel"), lax.axis_index("snp")
    half, me = lax.div(panel, HALF), lax.rem(panel, HALF)
    base = half * HALF
    z, ylo = lax.div(snp, 2), lax.rem(snp, 2)

    def peer(d):
        return lax.rem(me + d, HALF)

    def slab(d):
        return lax.rem(snp + d, 8)

    def deep(dz):
        return lax.rem(z + dz, 4)

    across = (lax.rem(panel + HALF, 2 * HALF), snp)
    beside = (panel, z * 2 + 1 - ylo)

    def copy(stage, i, src, dst, where):
        pltpu.make_async_remote_copy(
            src_ref=src, dst_ref=dst, send_sem=ssem.at[stage, i], recv_sem=rsem.at[stage, i],
            device_id=where, device_id_type=MESH,
        ).start()

    loads = [
        pltpu.make_async_copy(
            dosage_ref.at[:, pl.ds(i * rows, rows)], std.at[:, pl.ds(i * rows, rows)], load_sem.at[i]
        )
        for i in range(chunks)
    ]
    for load in loads:
        load.start()

    greeted = [(base + peer(d), snp) for d in range(1, 8)]
    greeted += [(base + peer(d), slab(d)) for d in range(1, 8)]
    greeted += [(panel, deep(dz) * 2 + ylo) for dz in (1, 2, 3)]
    greeted += [across, beside]
    barrier = pltpu.get_barrier_semaphore()
    for where in greeted:
        pl.semaphore_signal(barrier, inc=1, device_id=where, device_id_type=MESH)
    pl.semaphore_wait(barrier, len(greeted))

    freq = freq_ref[...]
    shift = 2.0 * freq
    scale = 1.0 / jnp.sqrt(2.0 * freq * (1.0 - freq))

    def span(i):
        return pl.ds(pl.multiple_of(i * rows, rows), rows)

    def spread(i):
        for d in ORDER:
            copy(0, i, std.at[peer(d), span(i)], pool.at[i, me], (base + peer(d), snp))

    def standardize(i, carry):
        pltpu.make_async_copy(
            dosage_ref.at[:, span(i)], std.at[:, span(i)], load_sem.at[i]
        ).wait()

        def one(l, c):
            value = (std[l, span(i), :].astype(jnp.float32) - shift) * scale
            std[l, span(i), :] = value.astype(jnp.bfloat16)
            return c

        lax.fori_loop(0, 8, one, 0)
        pool[i, me] = std[me, span(i), :]

        @pl.when(i < 2)
        def _():
            spread(i)

        return carry

    lax.fori_loop(0, chunks, standardize, 0)

    tables(plan_ref, step_ref, low_ref, colour_ref, to_ref, from_ref, rank_ref, 2 * HALF)
    for kind, (needs, gives) in enumerate(((from_ref, to_ref), (to_ref, from_ref))):

        def slots(j, carry, kind=kind, needs=needs, gives=gives):
            def pick(v, found):
                hit = (rank_ref[kind, base + v] == j) & (lax.div(gives[base + v], HALF) != half)
                return found + jnp.where(hit, v, 0)

            slot_ref[kind, j] = lax.fori_loop(0, HALF, pick, jnp.int32(0))
            source = needs[base + j]
            slot_ref[2 + kind, j] = jnp.where(
                lax.div(source, HALF) == half, lax.rem(source, HALF), HALF + rank_ref[kind, source]
            )
            return carry

        lax.fori_loop(0, HALF, slots, 0)
    origin = lax.rem(to_ref[panel], HALF)
    multiplier = 1.0 / math.sqrt(8192.0)

    def cross(stage, i, buf, keep, out, kind):
        keep[0:HALF] = buf[i, 0:HALF]
        for j in range(crossing):
            out[i, j] = keep[slot_ref[kind, j]]
        copy(stage, i, out.at[i], buf.at[i, pl.ds(HALF, crossing)], across)

    def arrive(stage, i, buf, keep, out, dst, kind):
        keep[...] = buf[i]
        for d in ORDER:
            w = peer(d)
            out[i, w] = keep[slot_ref[2 + kind, w]]
            copy(stage, i, out.at[i, w], dst.at[i, me], (base + w, snp))
        dst[i, me] = keep[slot_ref[2 + kind, me]]

    def step(t, carry):
        def stage(lag, first=0):
            return t - lag, (t >= lag + first) & (t < lag + chunks)

        i0, on = stage(0, 2)

        @pl.when(on)
        def _():
            spread(i0)

        i1, on = stage(1)

        @pl.when(on)
        def _():
            wait_for(pool.at[i1, pl.ds(0, 7)], rsem.at[0, i1])
            cross(1, i1, pool, held, cross_out, 0)

        i2, on = stage(2)

        @pl.when(on)
        def _():
            wait_for(cross_out.at[i2], rsem.at[1, i2])
            arrive(2, i2, pool, held, arr_out, partner, 0)

        i3, on = stage(3)

        @pl.when(on)
        def _():
            wait_for(partner.at[i3, pl.ds(0, 7)], rsem.at[2, i3])
            block = partner[i3].reshape(HALF * rows, 1024)
            for dz in (1, 2, 3, 0):
                owner = deep(dz) * 2
                for y in range(2):
                    product = lax.dot_general(
                        block, std[owner + y], (((1,), (1,)), ((), ())), preferred_element_type=jnp.float32
                    )
                    part[i3, owner + y] = (product * multiplier).astype(jnp.bfloat16)
                if dz:
                    copy(3, i3, part.at[i3, pl.ds(owner, 2)], zin.at[i3, dz - 1], (panel, owner + ylo))

        i4, on = stage(4)

        @pl.when(on)
        def _():
            wait_for(zin.at[i4], rsem.at[3, i4])

            def add(y):
                value = part[i4, z * 2 + y].astype(jnp.float32)
                for s in range(3):
                    value = value + zin[i4, s, y].astype(jnp.float32)
                return value

            yout[i4] = add(1 - ylo).astype(jnp.bfloat16)
            copy(4, i4, yout.at[i4], yin.at[i4], beside)
            total[:, span(i4)] = add(ylo).reshape(HALF, rows, 256)

        i5, on = stage(5)

        @pl.when(on)
        def _():
            wait_for(yin.at[i5], rsem.at[4, i5])
            value = total[:, span(i5)] + yin[i5].astype(jnp.float32).reshape(HALF, rows, 256)
            total[:, span(i5)] = value
            tout[i5] = value.astype(jnp.bfloat16)
            for d in ORDER:
                copy(5, i5, tout.at[i5, slab(d)], tpool.at[i5, me], (base + peer(d), slab(d)))
            tpool[i5, me] = tout[i5, snp]

        i6, on = stage(6)

        @pl.when(on)
        def _():
            wait_for(tpool.at[i6, pl.ds(0, 7)], rsem.at[5, i6])
            cross(6, i6, tpool, theld, tcross_out, 1)

        i7, on = stage(7)

        @pl.when(on)
        def _():
            wait_for(tcross_out.at[i7], rsem.at[6, i7])
            arrive(7, i7, tpool, theld, tarr_out, tin, 1)

        i8, on = stage(8)

        @pl.when(on)
        def _():
            wait_for(tin.at[i8, pl.ds(0, 7)], rsem.at[7, i8])
            theld[0:8] = tin[i8]
            for b in range(8):
                member = lax.rem(snp + origin - b + 8, 8)
                other_ref[span(i8), b * 256 : (b + 1) * 256] = theld[member]

        return carry

    lax.fori_loop(0, chunks + 8, step, 0)

    for b in range(8):
        own_ref[:, b * 256 : (b + 1) * 256] = total[b].T

    def drain(i, carry):
        for stage, ref in enumerate(
            (pool.at[i, pl.ds(0, 7)], cross_out.at[i], partner.at[i, pl.ds(0, 7)], zin.at[i],
             yin.at[i], tpool.at[i, pl.ds(0, 7)], tcross_out.at[i], tin.at[i, pl.ds(0, 7)])
        ):
            wait_for(ref, ssem.at[stage, i])
        return carry

    lax.fori_loop(0, chunks, drain, 0)


def tiles(dosage, freq, plan, chunks, crossing, collective_id):
    rows = 256 // chunks
    bf16 = jnp.bfloat16
    vmem, smem = pltpu.VMEM, pltpu.SMEM
    return pl.pallas_call(
        functools.partial(kernel, chunks, crossing),
        out_shape=(
            jax.ShapeDtypeStruct((256, 2048), jnp.float32),
            jax.ShapeDtypeStruct((256, 2048), bf16),
        ),
        in_specs=[
            pl.BlockSpec(memory_space=smem),
            pl.BlockSpec(memory_space=vmem),
            pl.BlockSpec(memory_space=pl.ANY),
        ],
        out_specs=(pl.BlockSpec(memory_space=vmem), pl.BlockSpec(memory_space=vmem)),
        scratch_shapes=[
            vmem((8, 256, 1024), bf16),
            vmem((chunks, HALF + crossing, rows, 1024), bf16),
            vmem((chunks, crossing, rows, 1024), bf16),
            vmem((chunks, HALF, rows, 1024), bf16),
            vmem((chunks, HALF, rows, 1024), bf16),
            vmem((chunks, 8, HALF * rows, 256), bf16),
            vmem((chunks, 3, 2, HALF * rows, 256), bf16),
            vmem((chunks, HALF * rows, 256), bf16),
            vmem((chunks, HALF * rows, 256), bf16),
            vmem((8, 256, 256), jnp.float32),
            vmem((chunks, 8, rows, 256), bf16),
            vmem((chunks, HALF + crossing, rows, 256), bf16),
            vmem((chunks, crossing, rows, 256), bf16),
            vmem((chunks, HALF, rows, 256), bf16),
            vmem((chunks, HALF, rows, 256), bf16),
            vmem((HALF + crossing, rows, 1024), bf16),
            vmem((HALF + crossing, rows, 256), bf16),
            smem((3, 16), jnp.int32),
            smem((3, 16), jnp.int32),
            smem((16,), jnp.int32),
            smem((16,), jnp.int32),
            smem((16,), jnp.int32),
            smem((2, 16), jnp.int32),
            smem((4, 8), jnp.int32),
            pltpu.SemaphoreType.DMA((chunks,)),
            pltpu.SemaphoreType.DMA((8, chunks)),
            pltpu.SemaphoreType.DMA((8, chunks)),
        ],
        compiler_params=pltpu.CompilerParams(
            collective_id=collective_id, has_side_effects=True, vmem_limit_bytes=60 << 20
        ),
        cost_estimate=pl.CostEstimate(flops=2 * 2048 * 2048 * 1024, bytes_accessed=10 << 20, transcendentals=0),
        name=f"tiles{crossing}",
    )(plan, freq, dosage)


def local(dosage, allele_freq, plan):
    dosage = dosage.reshape(8, 256, 1024)
    freq = allele_freq.reshape(1, 1024)
    own, other = tiles(dosage, freq, plan, 8, 8, 0)
    other = other.astype(jnp.float32)
    first, second = plan[0], plan[1]
    who = jnp.arange(16, dtype=jnp.int32)
    hot = lambda p: p[:, None] == who[None, :]
    take = lambda h, x: jnp.sum(jnp.where(h, x[None, :], 0), axis=1)
    jump = take(hot(first), second)
    low = jnp.minimum(who, jump)
    for _ in range(2):
        jump = take(hot(jump), jump)
        low = jnp.minimum(low, take(hot(jump), low))
    zero = low < take(hot(first), low)
    mine = jnp.sum(jnp.where(who == lax.axis_index("panel"), zero, False).astype(jnp.int32)) > 0
    return jnp.stack([jnp.where(mine, own, other), jnp.where(mine, other, own)], axis=0)


def solution(mesh):
    return jax.shard_map(
        local,
        mesh=mesh,
        in_specs=(P("panel", "snp"), P("snp"), P()),
        out_specs=P(None, ("panel", "snp"), None),
        check_vma=False,
    )
```

```python
import functools
import math

import jax
import jax.numpy as jnp
from jax import lax
from jax.experimental import pallas as pl
from jax.experimental.pallas import tpu as pltpu
from jax.sharding import PartitionSpec as P

MESH = pl.DeviceIdType.MESH
CHUNKS = 8
PRE = 0
SEQ=(0,1,2,3,4,5,6,7,8,9,10,11)
LAGS=(0,1,2,3,4,5,6,7,8,9,10)
TG = 2
EARLY = 2
HALF = 8
ORDER = (2, 6, 4, 3, 7, 5, 1)


def wait_for(ref, sem):
    pltpu.make_async_copy(ref, ref, sem).wait()


def tables(plan_ref, step_ref, low_ref, colour_ref, to_ref, from_ref, rank_ref, n):
    def start(v, carry):
        nxt = plan_ref[1, plan_ref[0, v]]
        step_ref[0, v] = nxt
        low_ref[0, v] = jnp.minimum(v, nxt)
        return carry

    lax.fori_loop(0, n, start, 0)
    for j in range(2):

        def double(v, carry, j=j):
            nxt = step_ref[j, step_ref[j, v]]
            step_ref[j + 1, v] = nxt
            low_ref[j + 1, v] = jnp.minimum(low_ref[j, v], low_ref[j, nxt])
            return carry

        lax.fori_loop(0, n, double, 0)

    def settle(v, carry):
        first, second = plan_ref[0, v], plan_ref[1, v]
        zero = low_ref[2, v] < low_ref[2, first]
        colour_ref[v] = jnp.where(zero, 0, 1)
        from_ref[v] = jnp.where(zero, first, second)
        to_ref[v] = jnp.where(zero, second, first)
        return carry

    lax.fori_loop(0, n, settle, 0)

    def ranks(v, carry):
        a, b = carry
        restart = lax.rem(v, HALF) == 0
        a, b = jnp.where(restart, 0, a), jnp.where(restart, 0, b)
        rank_ref[0, v] = a
        rank_ref[1, v] = b
        mine = lax.div(v, HALF)
        a = a + jnp.where(lax.div(to_ref[v], HALF) != mine, 1, 0)
        b = b + jnp.where(lax.div(from_ref[v], HALF) != mine, 1, 0)
        return a, b

    lax.fori_loop(0, n, ranks, (jnp.int32(0), jnp.int32(0)))


def kernel(
    chunks, crossing, plan_ref, freq_ref, dosage_ref, own_ref, other_ref, mine_ref,
    std, pool, cross_out, arr_out, partner, part, zfar, zsum, zin, yout, yin, total,
    tout, tpool, tcross_out, tarr_out, tin, held, theld,
    step_ref, low_ref, colour_ref, to_ref, from_ref, rank_ref, slot_ref,
    load_sem, ssem, rsem,
):
    rows = 256 // chunks
    panel, snp = lax.axis_index("panel"), lax.axis_index("snp")
    half, me = lax.div(panel, HALF), lax.rem(panel, HALF)
    base = half * HALF
    z, ylo = lax.div(snp, 2), lax.rem(snp, 2)

    def peer(d):
        return lax.rem(me + d, HALF)

    def slab(d):
        return lax.rem(snp + d, 8)

    def deep(dz):
        return lax.rem(z + dz, 4)

    across = (lax.rem(panel + HALF, 2 * HALF), snp)
    beside = (panel, z * 2 + 1 - ylo)

    def copy(stage, i, src, dst, where):
        pltpu.make_async_remote_copy(
            src_ref=src, dst_ref=dst, send_sem=ssem.at[stage, i], recv_sem=rsem.at[stage, i],
            device_id=where, device_id_type=MESH,
        ).start()

    greeted = [(base + peer(d), snp) for d in range(1, 8)]
    greeted += [(base + peer(d), slab(d)) for d in range(1, 8)]
    greeted += [(panel, deep(dz) * 2 + ylo) for dz in (1, 3)]
    greeted += [across, beside]
    barrier = pltpu.get_barrier_semaphore()
    for where in greeted:
        pl.semaphore_signal(barrier, inc=1, device_id=where, device_id_type=MESH)
    loads = [
        pltpu.make_async_copy(
            dosage_ref.at[:, pl.ds(i * rows, rows)], std.at[:, pl.ds(i * rows, rows)], load_sem.at[i]
        )
        for i in range(chunks)
    ]
    for load in loads:
        load.start()

    freq = freq_ref[...]
    shift = 2.0 * freq
    scale = 1.0 / jnp.sqrt(2.0 * freq * (1.0 - freq))

    def span(i):
        return pl.ds(pl.multiple_of(i * rows, rows), rows)

    def spread(i):
        for d in ORDER:
            copy(0, i, std.at[peer(d), span(i)], pool.at[i, me], (base + peer(d), snp))

    def standardize(i, carry):
        pltpu.make_async_copy(
            dosage_ref.at[:, span(i)], std.at[:, span(i)], load_sem.at[i]
        ).wait()

        def one(l, c):
            value = (std[l, span(i), :].astype(jnp.float32) - shift) * scale
            std[l, span(i), :] = value.astype(jnp.bfloat16)
            return c

        lax.fori_loop(0, 8, one, 0)
        pool[i, me] = std[me, span(i), :]

        return carry

    tables(plan_ref, step_ref, low_ref, colour_ref, to_ref, from_ref, rank_ref, 2 * HALF)
    for kind, (needs, gives) in enumerate(((from_ref, to_ref), (to_ref, from_ref))):

        def slots(j, carry, kind=kind, needs=needs, gives=gives):
            def pick(v, found):
                hit = (rank_ref[kind, base + v] == j) & (lax.div(gives[base + v], HALF) != half)
                return found + jnp.where(hit, v, 0)

            slot_ref[kind, j] = lax.fori_loop(0, HALF, pick, jnp.int32(0))
            source = needs[base + j]
            slot_ref[2 + kind, j] = jnp.where(
                lax.div(source, HALF) == half, lax.rem(source, HALF), HALF + rank_ref[kind, source]
            )
            return carry

        lax.fori_loop(0, HALF, slots, 0)
    lax.fori_loop(0, EARLY, standardize, 0)
    pl.semaphore_wait(barrier, len(greeted))

    for i in range(EARLY):
        spread(i)
    lax.fori_loop(EARLY, chunks, standardize, 0)

    mine_ref[...] = jnp.full((8, 128), colour_ref[panel], jnp.int32)
    origin = lax.rem(to_ref[panel], HALF)
    multiplier = 1.0 / math.sqrt(8192.0)

    def cross(stage, i, buf, keep, out, kind):
        keep[0:HALF] = buf[i, 0:HALF]
        for j in range(crossing):
            out[i, j] = keep[slot_ref[kind, j]]
        copy(stage, i, out.at[i], buf.at[i, pl.ds(HALF, crossing)], across)

    def arrive(stage, i, buf, keep, out, dst, kind):
        keep[...] = buf[i]
        for d in ORDER:
            w = peer(d)
            out[i, w] = keep[slot_ref[2 + kind, w]]
            copy(stage, i, out.at[i, w], dst.at[i, me], (base + w, snp))
        dst[i, me] = keep[slot_ref[2 + kind, me]]

    def step(t, carry):
        def stage(lag, first=0):
            return t - lag, (t >= lag + first) & (t < lag + chunks)

        def stage0():
            i0 = t + PRE

            @pl.when((i0 >= EARLY) & (i0 < chunks))
            def _():
                spread(i0)

        def stage1():
            i1, on = stage(LAGS[1])

            @pl.when(on)
            def _():
                wait_for(pool.at[i1, pl.ds(0, 7)], rsem.at[0, i1])
                cross(1, i1, pool, held, cross_out, 0)

        def stage2():
            i2, on = stage(LAGS[2])

            @pl.when(on)
            def _():
                wait_for(cross_out.at[i2], rsem.at[1, i2])
                arrive(2, i2, pool, held, arr_out, partner, 0)

        def stage3():
            i3, on = stage(LAGS[3])

            @pl.when(on)
            def _():
                wait_for(partner.at[i3, pl.ds(0, 7)], rsem.at[2, i3])
                block = partner[i3].reshape(HALF * rows, 1024)

                def multiply(owner, y):
                    product = lax.dot_general(
                        block, std[owner * 2 + y], (((1,), (1,)), ((), ())), preferred_element_type=jnp.float32
                    )
                    part[i3, owner * 2 + y] = (product * multiplier).astype(jnp.bfloat16)

                def give(stage, owner, y, dst, to):
                    copy(stage, i3, part.at[i3, owner * 2 + y], dst, (panel, to * 2 + ylo))

                after, before, far = deep(1), deep(3), deep(2)
                multiply(far, 0)
                give(3, far, 0, zfar.at[i3, 0], after)
                multiply(far, 1)
                give(3, far, 1, zfar.at[i3, 1], before)
                multiply(after, 1)
                give(4, after, 1, zin.at[i3, 1], after)
                multiply(before, 0)
                give(4, before, 0, zin.at[i3, 0], before)
                multiply(after, 0)
                multiply(before, 1)
                multiply(z, 0)
                multiply(z, 1)

        def stage4():
            i9, on = stage(LAGS[4])

            @pl.when(on)
            def _():
                wait_for(zfar.at[i9], rsem.at[3, i9])
                for y, to in ((0, deep(1)), (1, deep(3))):
                    value = part[i9, to * 2 + y].astype(jnp.float32) + zfar[i9, y].astype(jnp.float32)
                    zsum[i9, y] = value.astype(jnp.bfloat16)
                    copy(4, i9, zsum.at[i9, y], zin.at[i9, 2 + y], (panel, to * 2 + ylo))

        def stage5():
            i4, on = stage(LAGS[5])

            @pl.when(on)
            def _():
                wait_for(zin.at[i4], rsem.at[4, i4])

                def add(y):
                    return (
                        part[i4, z * 2 + y].astype(jnp.float32)
                        + zin[i4, y].astype(jnp.float32)
                        + zin[i4, 2 + y].astype(jnp.float32)
                    )

                yout[i4] = add(1 - ylo).astype(jnp.bfloat16)
                copy(5, i4, yout.at[i4], yin.at[i4], beside)
                total[:, span(i4)] = add(ylo).reshape(HALF, rows, 256)

        def stage6():
            i5, on = stage(LAGS[6])

            @pl.when(on)
            def _():
                wait_for(yin.at[i5], rsem.at[5, i5])
                value = total[:, span(i5)] + yin[i5].astype(jnp.float32).reshape(HALF, rows, 256)
                total[:, span(i5)] = value
                tout[lax.div(i5, TG), :, pl.ds(pl.multiple_of(lax.rem(i5, TG) * rows, rows), rows)] = value.astype(jnp.bfloat16)

        def group(lag):
            u = t - lag
            return lax.div(u, TG), (u >= 0) & (u < chunks) & (lax.rem(u, TG) == 0)

        def stage7():
            j, on = group(LAGS[7])

            @pl.when(on)
            def _():
                for d in ORDER:
                    copy(6, j, tout.at[j, slab(d)], tpool.at[j, me], (base + peer(d), slab(d)))
                tpool[j, me] = tout[j, snp]

        def stage8():
            j, on = group(LAGS[8])

            @pl.when(on)
            def _():
                wait_for(tpool.at[j, pl.ds(0, 7)], rsem.at[6, j])
                cross(7, j, tpool, theld, tcross_out, 1)

        def stage9():
            j, on = group(LAGS[9])

            @pl.when(on)
            def _():
                wait_for(tcross_out.at[j], rsem.at[7, j])
                arrive(8, j, tpool, theld, tarr_out, tin, 1)

        def stage10():
            j, on = group(LAGS[10])

            @pl.when(on)
            def _():
                wait_for(tin.at[j, pl.ds(0, 7)], rsem.at[8, j])
                theld[0:8] = tin[j]
                for b in range(8):
                    member = lax.rem(snp + origin - b + 8, 8)
                    other_ref[pl.ds(pl.multiple_of(j * TG * rows, TG * rows), TG * rows), b * 256 : (b + 1) * 256] = theld[member]

        def stage11():
            @pl.when(t == chunks + LAGS[6])
            def _():
                for b in range(8):
                    own_ref[:, b * 256 : (b + 1) * 256] = total[b].T

        fns = (stage0, stage1, stage2, stage3, stage4, stage5, stage6, stage7, stage8, stage9, stage10, stage11)
        for q in SEQ:
            fns[q]()
        return carry

    lax.fori_loop(0, chunks + LAGS[10], step, 0)

    def drain(i, carry):
        for stage, ref in enumerate(
            (pool.at[i, pl.ds(0, 7)], cross_out.at[i], partner.at[i, pl.ds(0, 7)], zfar.at[i], zin.at[i],
             yin.at[i])
        ):
            wait_for(ref, ssem.at[stage, i])
        return carry

    lax.fori_loop(0, chunks, drain, 0)

    def tdrain(j, carry):
        for stage, ref in enumerate((tpool.at[j, pl.ds(0, 7)], tcross_out.at[j], tin.at[j, pl.ds(0, 7)])):
            wait_for(ref, ssem.at[6 + stage, j])
        return carry

    lax.fori_loop(0, chunks // TG, tdrain, 0)


def tiles(dosage, freq, plan, chunks, crossing, collective_id):
    rows = 256 // chunks
    bf16 = jnp.bfloat16
    vmem, smem = pltpu.VMEM, pltpu.SMEM
    return pl.pallas_call(
        functools.partial(kernel, chunks, crossing),
        out_shape=(
            jax.ShapeDtypeStruct((256, 2048), jnp.float32),
            jax.ShapeDtypeStruct((256, 2048), bf16),
            jax.ShapeDtypeStruct((8, 128), jnp.int32),
        ),
        in_specs=[
            pl.BlockSpec(memory_space=smem),
            pl.BlockSpec(memory_space=vmem),
            pl.BlockSpec(memory_space=pl.ANY),
        ],
        out_specs=(pl.BlockSpec(memory_space=vmem),) * 3,
        scratch_shapes=[
            vmem((8, 256, 1024), bf16),
            vmem((chunks, HALF + crossing, rows, 1024), bf16),
            vmem((chunks, crossing, rows, 1024), bf16),
            vmem((chunks, HALF, rows, 1024), bf16),
            vmem((chunks, HALF, rows, 1024), bf16),
            vmem((chunks, 8, HALF * rows, 256), bf16),
            vmem((chunks, 2, HALF * rows, 256), bf16),
            vmem((chunks, 2, HALF * rows, 256), bf16),
            vmem((chunks, 4, HALF * rows, 256), bf16),
            vmem((chunks, HALF * rows, 256), bf16),
            vmem((chunks, HALF * rows, 256), bf16),
            vmem((8, 256, 256), jnp.float32),
            vmem((chunks // TG, 8, TG * rows, 256), bf16),
            vmem((chunks // TG, HALF + crossing, TG * rows, 256), bf16),
            vmem((chunks // TG, crossing, TG * rows, 256), bf16),
            vmem((chunks // TG, HALF, TG * rows, 256), bf16),
            vmem((chunks // TG, HALF, TG * rows, 256), bf16),
            vmem((HALF + crossing, rows, 1024), bf16),
            vmem((HALF + crossing, TG * rows, 256), bf16),
            smem((3, 16), jnp.int32),
            smem((3, 16), jnp.int32),
            smem((16,), jnp.int32),
            smem((16,), jnp.int32),
            smem((16,), jnp.int32),
            smem((2, 16), jnp.int32),
            smem((4, 8), jnp.int32),
            pltpu.SemaphoreType.DMA((chunks,)),
            pltpu.SemaphoreType.DMA((9, chunks)),
            pltpu.SemaphoreType.DMA((9, chunks)),
        ],
        compiler_params=pltpu.CompilerParams(
            collective_id=collective_id, has_side_effects=True, vmem_limit_bytes=60 << 20
        ),
        cost_estimate=pl.CostEstimate(flops=2 * 2048 * 2048 * 1024, bytes_accessed=10 << 20, transcendentals=0),
        name=f"tiles{crossing}",
    )(plan, freq, dosage)


def local(dosage, allele_freq, plan):
    dosage = dosage.reshape(8, 256, 1024)
    freq = allele_freq.reshape(1, 1024)
    half = jnp.arange(16, dtype=jnp.int32)[None, :] // HALF
    crossings = jnp.sum((plan // HALF != half).astype(jnp.int32))
    few = functools.partial(tiles, chunks=CHUNKS, crossing=5, collective_id=1)
    every = functools.partial(tiles, chunks=CHUNKS, crossing=8, collective_id=0)
    own, other, colour = lax.cond(crossings <= 20, few, every, dosage, freq, plan)
    first = lax.broadcasted_iota(jnp.int32, (2, 256, 2048), 0) == colour[0, 0]
    return jnp.where(first, own[None], other[None].astype(jnp.float32))


def solution(mesh):
    return jax.shard_map(
        local,
        mesh=mesh,
        in_specs=(P("panel", "snp"), P("snp"), P()),
        out_specs=P(None, ("panel", "snp"), None),
        check_vma=False,
    )
```

```python
import functools
import math

import jax
import jax.numpy as jnp
from jax import lax
from jax.experimental import pallas as pl
from jax.experimental.pallas import tpu as pltpu
from jax.sharding import PartitionSpec as P

MESH = pl.DeviceIdType.MESH
CHUNKS = 8
PRE = 0
SEQ = (0, 1, 2, 3, 4, 5, 6, 7, 8, 9, 10, 11)
LAGS = (0, 1, 2, 3, 4, 5, 6, 7, 8, 9, 10)
TG = 2
EARLY = 2
BLOCKS = 2
HALF = 8
ORDER = (1, 7, 3, 5, 2, 6, 4)


def wait_for(ref, sem):
    pltpu.make_async_copy(ref, ref, sem).wait()


def tables(plan_ref, step_ref, low_ref, colour_ref, to_ref, from_ref, rank_ref, n):
    def start(v, carry):
        nxt = plan_ref[1, plan_ref[0, v]]
        step_ref[0, v] = nxt
        low_ref[0, v] = jnp.minimum(v, nxt)
        return carry

    lax.fori_loop(0, n, start, 0)
    for j in range(2):

        def double(v, carry, j=j):
            nxt = step_ref[j, step_ref[j, v]]
            step_ref[j + 1, v] = nxt
            low_ref[j + 1, v] = jnp.minimum(low_ref[j, v], low_ref[j, nxt])
            return carry

        lax.fori_loop(0, n, double, 0)

    def settle(v, carry):
        first, second = plan_ref[0, v], plan_ref[1, v]
        zero = low_ref[2, v] < low_ref[2, first]
        colour_ref[v] = jnp.where(zero, 0, 1)
        from_ref[v] = jnp.where(zero, first, second)
        to_ref[v] = jnp.where(zero, second, first)
        return carry

    lax.fori_loop(0, n, settle, 0)

    def ranks(v, carry):
        a, b = carry
        restart = lax.rem(v, HALF) == 0
        a, b = jnp.where(restart, 0, a), jnp.where(restart, 0, b)
        rank_ref[0, v] = a
        rank_ref[1, v] = b
        mine = lax.div(v, HALF)
        a = a + jnp.where(lax.div(to_ref[v], HALF) != mine, 1, 0)
        b = b + jnp.where(lax.div(from_ref[v], HALF) != mine, 1, 0)
        return a, b

    lax.fori_loop(0, n, ranks, (jnp.int32(0), jnp.int32(0)))


def kernel(
    chunks, crossing, plan_ref, freq_ref, dosage_ref, own_ref, other_ref, mine_ref,
    std, pool, cross_out, arr_out, partner, part, zfar, zsum, zin, yout, yin, total,
    tout, tpool, tcross_out, tarr_out, tin, held, theld,
    step_ref, low_ref, colour_ref, to_ref, from_ref, rank_ref, slot_ref,
    load_sem, ssem, rsem,
):
    rows = 256 // chunks
    panel, snp = lax.axis_index("panel"), lax.axis_index("snp")
    half, me = lax.div(panel, HALF), lax.rem(panel, HALF)
    base = half * HALF
    z, ylo = lax.div(snp, 2), lax.rem(snp, 2)
    turn = lax.rem(me, 2)

    def peer(d):
        return lax.rem(me + d + turn * (HALF - 2 * d), HALF)

    def slab(d):
        return lax.rem(snp + d + turn * (8 - 2 * d), 8)

    def deep(dz):
        return lax.rem(z + dz, 4)

    across = (lax.rem(panel + HALF, 2 * HALF), snp)
    beside = (panel, z * 2 + 1 - ylo)

    def copy(stage, i, src, dst, where):
        pltpu.make_async_remote_copy(
            src_ref=src, dst_ref=dst, send_sem=ssem.at[stage, i], recv_sem=rsem.at[stage, i],
            device_id=where, device_id_type=MESH,
        ).start()

    greeted = [(base + peer(d), snp) for d in range(1, 8)]
    greeted += [(base + peer(d), slab(d)) for d in range(1, 8)]
    greeted += [(panel, deep(dz) * 2 + ylo) for dz in (1, 3)]
    greeted += [across, beside]
    barrier = pltpu.get_barrier_semaphore()
    for where in greeted:
        pl.semaphore_signal(barrier, inc=1, device_id=where, device_id_type=MESH)
    loads = [
        pltpu.make_async_copy(
            dosage_ref.at[:, pl.ds(i * rows, rows)], std.at[:, pl.ds(i * rows, rows)], load_sem.at[i]
        )
        for i in range(chunks)
    ]
    for load in loads:
        load.start()

    freq = freq_ref[...]
    shift = 2.0 * freq
    scale = 1.0 / jnp.sqrt(2.0 * freq * (1.0 - freq))

    def span(i):
        return pl.ds(pl.multiple_of(i * rows, rows), rows)

    def spread(i):
        for d in ORDER:
            copy(0, i, std.at[peer(d), span(i)], pool.at[i, me], (base + peer(d), snp))

    def standardize(i, carry):
        pltpu.make_async_copy(
            dosage_ref.at[:, span(i)], std.at[:, span(i)], load_sem.at[i]
        ).wait()

        def one(l, c):
            value = (std[l, span(i), :].astype(jnp.float32) - shift) * scale
            std[l, span(i), :] = value.astype(jnp.bfloat16)
            return c

        lax.fori_loop(0, 8, one, 0)
        pool[i, me] = std[me, span(i), :]

        return carry

    tables(plan_ref, step_ref, low_ref, colour_ref, to_ref, from_ref, rank_ref, 2 * HALF)
    for kind, (needs, gives) in enumerate(((from_ref, to_ref), (to_ref, from_ref))):

        def slots(j, carry, kind=kind, needs=needs, gives=gives):
            def pick(v, found):
                hit = (rank_ref[kind, base + v] == j) & (lax.div(gives[base + v], HALF) != half)
                return found + jnp.where(hit, v, 0)

            slot_ref[kind, j] = lax.fori_loop(0, HALF, pick, jnp.int32(0))
            source = needs[base + j]
            slot_ref[2 + kind, j] = jnp.where(
                lax.div(source, HALF) == half, lax.rem(source, HALF), HALF + rank_ref[kind, source]
            )
            return carry

        lax.fori_loop(0, HALF, slots, 0)
    lax.fori_loop(0, EARLY, standardize, 0)
    pl.semaphore_wait(barrier, len(greeted))

    for i in range(EARLY):
        spread(i)
    lax.fori_loop(EARLY, chunks, standardize, 0)

    mine_ref[...] = jnp.full((8, 128), colour_ref[panel], jnp.int32)
    origin = lax.rem(to_ref[panel], HALF)
    multiplier = 1.0 / math.sqrt(8192.0)

    def cross(stage, i, buf, keep, out, kind):
        keep[0:HALF] = buf[i, 0:HALF]
        for j in range(crossing):
            out[i, j] = keep[slot_ref[kind, j]]
        copy(stage, i, out.at[i], buf.at[i, pl.ds(HALF, crossing)], across)

    def arrive(stage, i, buf, keep, out, dst, kind):
        keep[...] = buf[i]
        for d in ORDER:
            w = peer(d)
            out[i, w] = keep[slot_ref[2 + kind, w]]
            copy(stage, i, out.at[i, w], dst.at[i, me], (base + w, snp))
        dst[i, me] = keep[slot_ref[2 + kind, me]]

    def step(t, carry):
        def stage(lag, first=0):
            return t - lag, (t >= lag + first) & (t < lag + chunks)

        def stage0():
            i0 = t + PRE

            @pl.when((i0 >= EARLY) & (i0 < chunks))
            def _():
                spread(i0)

        def stage1():
            i1, on = stage(LAGS[1])

            @pl.when(on)
            def _():
                wait_for(pool.at[i1, pl.ds(0, 7)], rsem.at[0, i1])
                cross(1, i1, pool, held, cross_out, 0)

        def stage2():
            i2, on = stage(LAGS[2])

            @pl.when(on)
            def _():
                wait_for(cross_out.at[i2], rsem.at[1, i2])
                arrive(2, i2, pool, held, arr_out, partner, 0)

        def stage3():
            i3, on = stage(LAGS[3])

            @pl.when(on)
            def _():
                wait_for(partner.at[i3, pl.ds(0, 7)], rsem.at[2, i3])
                block = partner[i3].reshape(HALF * rows, 1024)

                def multiply(owner, y):
                    product = lax.dot_general(
                        block, std[owner * 2 + y], (((1,), (1,)), ((), ())), preferred_element_type=jnp.float32
                    )
                    part[i3, owner * 2 + y] = (product * multiplier).astype(jnp.bfloat16)

                def give(stage, owner, y, dst, to):
                    copy(stage, i3, part.at[i3, owner * 2 + y], dst, (panel, to * 2 + ylo))

                after, before, far = deep(1), deep(3), deep(2)
                multiply(far, 0)
                give(3, far, 0, zfar.at[i3, 0], after)
                multiply(far, 1)
                give(3, far, 1, zfar.at[i3, 1], before)
                multiply(after, 1)
                give(4, after, 1, zin.at[i3, 1], after)
                multiply(before, 0)
                give(4, before, 0, zin.at[i3, 0], before)
                multiply(after, 0)
                multiply(before, 1)
                multiply(z, 0)
                multiply(z, 1)

        def stage4():
            i9, on = stage(LAGS[4])

            @pl.when(on)
            def _():
                wait_for(zfar.at[i9], rsem.at[3, i9])
                for y, to in ((0, deep(1)), (1, deep(3))):
                    value = part[i9, to * 2 + y].astype(jnp.float32) + zfar[i9, y].astype(jnp.float32)
                    zsum[i9, y] = value.astype(jnp.bfloat16)
                    copy(4, i9, zsum.at[i9, y], zin.at[i9, 2 + y], (panel, to * 2 + ylo))

        def stage5():
            i4, on = stage(LAGS[5])

            @pl.when(on)
            def _():
                wait_for(zin.at[i4], rsem.at[4, i4])

                def add(y):
                    return (
                        part[i4, z * 2 + y].astype(jnp.float32)
                        + zin[i4, y].astype(jnp.float32)
                        + zin[i4, 2 + y].astype(jnp.float32)
                    )

                yout[i4] = add(1 - ylo).astype(jnp.bfloat16)
                copy(5, i4, yout.at[i4], yin.at[i4], beside)
                total[:, span(i4)] = add(ylo).reshape(HALF, rows, 256)

        def stage6():
            i5, on = stage(LAGS[6])

            @pl.when(on)
            def _():
                wait_for(yin.at[i5], rsem.at[5, i5])
                value = total[:, span(i5)] + yin[i5].astype(jnp.float32).reshape(HALF, rows, 256)
                total[:, span(i5)] = value
                tout[lax.div(i5, TG), :, pl.ds(pl.multiple_of(lax.rem(i5, TG) * rows, rows), rows)] = value.astype(jnp.bfloat16)

        def group(lag):
            u = t - lag
            return lax.div(u, TG), (u >= 0) & (u < chunks) & (lax.rem(u, TG) == 0)

        def stage7():
            j, on = group(LAGS[7])

            @pl.when(on)
            def _():
                for d in ORDER:
                    copy(6, j, tout.at[j, slab(d)], tpool.at[j, me], (base + peer(d), slab(d)))
                tpool[j, me] = tout[j, snp]

        def stage8():
            j, on = group(LAGS[8])

            @pl.when(on)
            def _():
                wait_for(tpool.at[j, pl.ds(0, 7)], rsem.at[6, j])
                cross(7, j, tpool, theld, tcross_out, 1)

        def stage9():
            j, on = group(LAGS[9])

            @pl.when(on)
            def _():
                wait_for(tcross_out.at[j], rsem.at[7, j])
                arrive(8, j, tpool, theld, tarr_out, tin, 1)

        def stage10():
            j, on = group(LAGS[10])

            @pl.when(on)
            def _():
                wait_for(tin.at[j, pl.ds(0, 7)], rsem.at[8, j])
                theld[0:8] = tin[j]
                for b in range(8):
                    member = lax.rem(snp + origin - b + 8, 8)
                    other_ref[pl.ds(pl.multiple_of(j * TG * rows, TG * rows), TG * rows), b * 256 : (b + 1) * 256] = theld[member]

        def stage11():
            @pl.when(t == chunks + LAGS[6])
            def _():
                for b in range(8):
                    own_ref[:, b * 256 : (b + 1) * 256] = total[b].T

        fns = (stage0, stage1, stage2, stage3, stage4, stage5, stage6, stage7, stage8, stage9, stage10, stage11)
        for q in SEQ:
            fns[q]()
        return carry

    lax.fori_loop(0, chunks + LAGS[10], step, 0)

    def drain(i, carry):
        for stage, ref in enumerate(
            (pool.at[i, pl.ds(0, 7)], cross_out.at[i], partner.at[i, pl.ds(0, 7)], zfar.at[i], zin.at[i],
             yin.at[i])
        ):
            wait_for(ref, ssem.at[stage, i])
        return carry

    lax.fori_loop(0, chunks, drain, 0)

    def tdrain(j, carry):
        for stage, ref in enumerate((tpool.at[j, pl.ds(0, 7)], tcross_out.at[j], tin.at[j, pl.ds(0, 7)])):
            wait_for(ref, ssem.at[6 + stage, j])
        return carry

    lax.fori_loop(0, chunks // TG, tdrain, 0)


def tiles(dosage, freq, plan, chunks, crossing, collective_id):
    rows = 256 // chunks
    bf16 = jnp.bfloat16
    vmem, smem = pltpu.VMEM, pltpu.SMEM
    return pl.pallas_call(
        functools.partial(kernel, chunks, crossing),
        out_shape=(
            jax.ShapeDtypeStruct((256, 2048), jnp.float32),
            jax.ShapeDtypeStruct((256, 2048), bf16),
            jax.ShapeDtypeStruct((8, 128), jnp.int32),
        ),
        in_specs=[
            pl.BlockSpec(memory_space=smem),
            pl.BlockSpec(memory_space=vmem),
            pl.BlockSpec(memory_space=pl.ANY),
        ],
        out_specs=(pl.BlockSpec(memory_space=vmem),) * 3,
        scratch_shapes=[
            vmem((8, 256, 1024), bf16),
            vmem((chunks, HALF + crossing, rows, 1024), bf16),
            vmem((chunks, crossing, rows, 1024), bf16),
            vmem((chunks, HALF, rows, 1024), bf16),
            vmem((chunks, HALF, rows, 1024), bf16),
            vmem((chunks, 8, HALF * rows, 256), bf16),
            vmem((chunks, 2, HALF * rows, 256), bf16),
            vmem((chunks, 2, HALF * rows, 256), bf16),
            vmem((chunks, 4, HALF * rows, 256), bf16),
            vmem((chunks, HALF * rows, 256), bf16),
            vmem((chunks, HALF * rows, 256), bf16),
            vmem((8, 256, 256), jnp.float32),
            vmem((chunks // TG, 8, TG * rows, 256), bf16),
            vmem((chunks // TG, HALF + crossing, TG * rows, 256), bf16),
            vmem((chunks // TG, crossing, TG * rows, 256), bf16),
            vmem((chunks // TG, HALF, TG * rows, 256), bf16),
            vmem((chunks // TG, HALF, TG * rows, 256), bf16),
            vmem((HALF + crossing, rows, 1024), bf16),
            vmem((HALF + crossing, TG * rows, 256), bf16),
            smem((3, 16), jnp.int32),
            smem((3, 16), jnp.int32),
            smem((16,), jnp.int32),
            smem((16,), jnp.int32),
            smem((16,), jnp.int32),
            smem((2, 16), jnp.int32),
            smem((4, 8), jnp.int32),
            pltpu.SemaphoreType.DMA((chunks,)),
            pltpu.SemaphoreType.DMA((9, chunks)),
            pltpu.SemaphoreType.DMA((9, chunks)),
        ],
        compiler_params=pltpu.CompilerParams(
            collective_id=collective_id, has_side_effects=True, vmem_limit_bytes=60 << 20
        ),
        cost_estimate=pl.CostEstimate(flops=2 * 2048 * 2048 * 1024, bytes_accessed=10 << 20, transcendentals=0),
        name=f"tiles{crossing}",
    )(plan, freq, dosage)


def place(colour_ref, own_ref, other_ref, out_ref):
    own, other = own_ref[...], other_ref[...].astype(jnp.float32)
    first = colour_ref[0, 0] == 0
    out_ref[0] = jnp.where(first, own, other)
    out_ref[1] = jnp.where(first, other, own)


def local(dosage, allele_freq, plan):
    dosage = dosage.reshape(8, 256, 1024)
    freq = allele_freq.reshape(1, 1024)
    upper = jnp.arange(2 * HALF, dtype=jnp.int32)[None, :] >= HALF
    crossings = jnp.sum(((plan >= HALF) != upper).astype(jnp.int32))
    few, some, every = (
        functools.partial(tiles, chunks=CHUNKS, crossing=crossing, collective_id=i)
        for i, crossing in enumerate((5, 6, 8))
    )

    def more(*operands):
        return lax.cond(crossings <= 24, some, every, *operands)

    own, other, colour = lax.cond(crossings <= 20, few, more, dosage, freq, plan)
    return pl.pallas_call(
        place,
        out_shape=jax.ShapeDtypeStruct((2, 256, 2048), jnp.float32),
        grid=(BLOCKS,),
        in_specs=[
            pl.BlockSpec(memory_space=pltpu.SMEM),
            pl.BlockSpec((256 // BLOCKS, 2048), lambda i: (i, 0)),
            pl.BlockSpec((256 // BLOCKS, 2048), lambda i: (i, 0)),
        ],
        out_specs=pl.BlockSpec((2, 256 // BLOCKS, 2048), lambda i: (0, i, 0)),
        name="place",
    )(colour, own, other)


def solution(mesh):
    return jax.shard_map(
        local,
        mesh=mesh,
        in_specs=(P("panel", "snp"), P("snp"), P()),
        out_specs=P(None, ("panel", "snp"), None),
        check_vma=False,
    )
```

```python
import functools
import math

import jax
import jax.numpy as jnp
from jax import lax
from jax.experimental import pallas as pl
from jax.experimental.pallas import tpu as pltpu
from jax.sharding import PartitionSpec as P

MESH = pl.DeviceIdType.MESH
CHUNKS = 8
PRE = 0
SEQ = (0, 1, 2, 3, 4, 5, 6, 7, 8, 9, 10, 11)
LAGS = (0, 1, 2, 3, 4, 5, 6, 6, 7, 8, 9)
TG = 1
EARLY = 2
BLOCKS = 2
HALF = 8
ORDER = (1, 7, 3, 5, 2, 6, 4)


def wait_for(ref, sem):
    pltpu.make_async_copy(ref, ref, sem).wait()


def tables(plan_ref, step_ref, low_ref, colour_ref, to_ref, from_ref, rank_ref, n):
    def start(v, carry):
        nxt = plan_ref[1, plan_ref[0, v]]
        step_ref[0, v] = nxt
        low_ref[0, v] = jnp.minimum(v, nxt)
        return carry

    lax.fori_loop(0, n, start, 0)
    for j in range(2):

        def double(v, carry, j=j):
            nxt = step_ref[j, step_ref[j, v]]
            step_ref[j + 1, v] = nxt
            low_ref[j + 1, v] = jnp.minimum(low_ref[j, v], low_ref[j, nxt])
            return carry

        lax.fori_loop(0, n, double, 0)

    def settle(v, carry):
        first, second = plan_ref[0, v], plan_ref[1, v]
        zero = low_ref[2, v] < low_ref[2, first]
        colour_ref[v] = jnp.where(zero, 0, 1)
        from_ref[v] = jnp.where(zero, first, second)
        to_ref[v] = jnp.where(zero, second, first)
        return carry

    lax.fori_loop(0, n, settle, 0)

    def ranks(v, carry):
        a, b = carry
        restart = lax.rem(v, HALF) == 0
        a, b = jnp.where(restart, 0, a), jnp.where(restart, 0, b)
        rank_ref[0, v] = a
        rank_ref[1, v] = b
        mine = lax.div(v, HALF)
        a = a + jnp.where(lax.div(to_ref[v], HALF) != mine, 1, 0)
        b = b + jnp.where(lax.div(from_ref[v], HALF) != mine, 1, 0)
        return a, b

    lax.fori_loop(0, n, ranks, (jnp.int32(0), jnp.int32(0)))


def kernel(
    chunks, crossing, plan_ref, freq_ref, dosage_ref, own_ref, other_ref, mine_ref,
    std, pool, cross_out, arr_out, partner, part, zfar, zsum, zin, yout, yin, total,
    tout, tpool, tcross_out, tarr_out, tin, held, theld,
    step_ref, low_ref, colour_ref, to_ref, from_ref, rank_ref, slot_ref,
    load_sem, ssem, rsem,
):
    rows = 256 // chunks
    panel, snp = lax.axis_index("panel"), lax.axis_index("snp")
    half, me = lax.div(panel, HALF), lax.rem(panel, HALF)
    base = half * HALF
    z, ylo = lax.div(snp, 2), lax.rem(snp, 2)
    turn = lax.rem(me, 2)

    def peer(d):
        return lax.rem(me + d + turn * (HALF - 2 * d), HALF)

    def slab(d):
        return lax.rem(snp + d + turn * (8 - 2 * d), 8)

    def deep(dz):
        return lax.rem(z + dz, 4)

    across = (lax.rem(panel + HALF, 2 * HALF), snp)
    beside = (panel, z * 2 + 1 - ylo)

    def copy(stage, i, src, dst, where):
        pltpu.make_async_remote_copy(
            src_ref=src, dst_ref=dst, send_sem=ssem.at[stage, i], recv_sem=rsem.at[stage, i],
            device_id=where, device_id_type=MESH,
        ).start()

    greeted = [(base + peer(d), snp) for d in range(1, 8)]
    greeted += [(base + peer(d), slab(d)) for d in range(1, 8)]
    greeted += [(panel, deep(dz) * 2 + ylo) for dz in (1, 3)]
    greeted += [across, beside]
    barrier = pltpu.get_barrier_semaphore()
    for where in greeted:
        pl.semaphore_signal(barrier, inc=1, device_id=where, device_id_type=MESH)
    loads = [
        pltpu.make_async_copy(
            dosage_ref.at[:, pl.ds(i * rows, rows)], std.at[:, pl.ds(i * rows, rows)], load_sem.at[i]
        )
        for i in range(chunks)
    ]
    for load in loads:
        load.start()

    freq = freq_ref[...]
    shift = 2.0 * freq
    scale = 1.0 / jnp.sqrt(2.0 * freq * (1.0 - freq))

    def span(i):
        return pl.ds(pl.multiple_of(i * rows, rows), rows)

    def spread(i):
        for d in ORDER:
            copy(0, i, std.at[peer(d), span(i)], pool.at[i, me], (base + peer(d), snp))

    def standardize(i, carry):
        pltpu.make_async_copy(
            dosage_ref.at[:, span(i)], std.at[:, span(i)], load_sem.at[i]
        ).wait()

        def one(l, c):
            value = (std[l, span(i), :].astype(jnp.float32) - shift) * scale
            std[l, span(i), :] = value.astype(jnp.bfloat16)
            return c

        lax.fori_loop(0, 8, one, 0)
        pool[i, me] = std[me, span(i), :]

        return carry

    tables(plan_ref, step_ref, low_ref, colour_ref, to_ref, from_ref, rank_ref, 2 * HALF)
    for kind, (needs, gives) in enumerate(((from_ref, to_ref), (to_ref, from_ref))):

        def slots(j, carry, kind=kind, needs=needs, gives=gives):
            def pick(v, found):
                hit = (rank_ref[kind, base + v] == j) & (lax.div(gives[base + v], HALF) != half)
                return found + jnp.where(hit, v, 0)

            slot_ref[kind, j] = lax.fori_loop(0, HALF, pick, jnp.int32(0))
            source = needs[base + j]
            slot_ref[2 + kind, j] = jnp.where(
                lax.div(source, HALF) == half, lax.rem(source, HALF), HALF + rank_ref[kind, source]
            )
            return carry

        lax.fori_loop(0, HALF, slots, 0)
    lax.fori_loop(0, EARLY, standardize, 0)
    pl.semaphore_wait(barrier, len(greeted))

    for i in range(EARLY):
        spread(i)
    lax.fori_loop(EARLY, chunks, standardize, 0)

    mine_ref[...] = jnp.full((8, 128), colour_ref[panel], jnp.int32)
    origin = lax.rem(to_ref[panel], HALF)
    multiplier = 1.0 / math.sqrt(8192.0)

    def cross(stage, i, buf, keep, out, kind):
        keep[0:HALF] = buf[i, 0:HALF]
        for j in range(crossing):
            out[i, j] = keep[slot_ref[kind, j]]
        copy(stage, i, out.at[i], buf.at[i, pl.ds(HALF, crossing)], across)

    def arrive(stage, i, buf, keep, out, dst, kind):
        keep[...] = buf[i]
        for d in ORDER:
            w = peer(d)
            out[i, w] = keep[slot_ref[2 + kind, w]]
            copy(stage, i, out.at[i, w], dst.at[i, me], (base + w, snp))
        dst[i, me] = keep[slot_ref[2 + kind, me]]

    def step(t, carry):
        def stage(lag, first=0):
            return t - lag, (t >= lag + first) & (t < lag + chunks)

        def stage0():
            i0 = t + PRE

            @pl.when((i0 >= EARLY) & (i0 < chunks))
            def _():
                spread(i0)

        def stage1():
            i1, on = stage(LAGS[1])

            @pl.when(on)
            def _():
                wait_for(pool.at[i1, pl.ds(0, 7)], rsem.at[0, i1])
                cross(1, i1, pool, held, cross_out, 0)

        def stage2():
            i2, on = stage(LAGS[2])

            @pl.when(on)
            def _():
                wait_for(cross_out.at[i2], rsem.at[1, i2])
                arrive(2, i2, pool, held, arr_out, partner, 0)

        def stage3():
            i3, on = stage(LAGS[3])

            @pl.when(on)
            def _():
                wait_for(partner.at[i3, pl.ds(0, 7)], rsem.at[2, i3])
                block = partner[i3].reshape(HALF * rows, 1024)

                def multiply(owner, y):
                    product = lax.dot_general(
                        block, std[owner * 2 + y], (((1,), (1,)), ((), ())), preferred_element_type=jnp.float32
                    )
                    part[i3, owner * 2 + y] = (product * multiplier).astype(jnp.bfloat16)

                def give(stage, owner, y, dst, to):
                    copy(stage, i3, part.at[i3, owner * 2 + y], dst, (panel, to * 2 + ylo))

                after, before, far = deep(1), deep(3), deep(2)
                multiply(far, 0)
                give(3, far, 0, zfar.at[i3, 0], after)
                multiply(far, 1)
                give(3, far, 1, zfar.at[i3, 1], before)
                multiply(after, 1)
                give(4, after, 1, zin.at[i3, 1], after)
                multiply(before, 0)
                give(4, before, 0, zin.at[i3, 0], before)
                multiply(after, 0)
                multiply(before, 1)
                multiply(z, 0)
                multiply(z, 1)

        def stage4():
            i9, on = stage(LAGS[4])

            @pl.when(on)
            def _():
                wait_for(zfar.at[i9], rsem.at[3, i9])
                for y, to in ((0, deep(1)), (1, deep(3))):
                    value = part[i9, to * 2 + y].astype(jnp.float32) + zfar[i9, y].astype(jnp.float32)
                    zsum[i9, y] = value.astype(jnp.bfloat16)
                    copy(4, i9, zsum.at[i9, y], zin.at[i9, 2 + y], (panel, to * 2 + ylo))

        def stage5():
            i4, on = stage(LAGS[5])

            @pl.when(on)
            def _():
                wait_for(zin.at[i4], rsem.at[4, i4])

                def add(y):
                    return (
                        part[i4, z * 2 + y].astype(jnp.float32)
                        + zin[i4, y].astype(jnp.float32)
                        + zin[i4, 2 + y].astype(jnp.float32)
                    )

                yout[i4] = add(1 - ylo).astype(jnp.bfloat16)
                copy(5, i4, yout.at[i4], yin.at[i4], beside)
                total[:, span(i4)] = add(ylo).reshape(HALF, rows, 256)

        def stage6():
            i5, on = stage(LAGS[6])

            @pl.when(on)
            def _():
                wait_for(yin.at[i5], rsem.at[5, i5])
                value = total[:, span(i5)] + yin[i5].astype(jnp.float32).reshape(HALF, rows, 256)
                total[:, span(i5)] = value
                tout[lax.div(i5, TG), :, pl.ds(pl.multiple_of(lax.rem(i5, TG) * rows, rows), rows)] = value.astype(jnp.bfloat16)

        def group(lag):
            u = t - lag
            return lax.div(u, TG), (u >= 0) & (u < chunks) & (lax.rem(u, TG) == 0)

        def stage7():
            j, on = group(LAGS[7])

            @pl.when(on)
            def _():
                for d in ORDER:
                    copy(6, j, tout.at[j, slab(d)], tpool.at[j, me], (base + peer(d), slab(d)))
                tpool[j, me] = tout[j, snp]

        def stage8():
            j, on = group(LAGS[8])

            @pl.when(on)
            def _():
                wait_for(tpool.at[j, pl.ds(0, 7)], rsem.at[6, j])
                cross(7, j, tpool, theld, tcross_out, 1)

        def stage9():
            j, on = group(LAGS[9])

            @pl.when(on)
            def _():
                wait_for(tcross_out.at[j], rsem.at[7, j])
                arrive(8, j, tpool, theld, tarr_out, tin, 1)

        def stage10():
            j, on = group(LAGS[10])

            @pl.when(on)
            def _():
                wait_for(tin.at[j, pl.ds(0, 7)], rsem.at[8, j])
                theld[0:8] = tin[j]
                for b in range(8):
                    member = lax.rem(snp + origin - b + 8, 8)
                    other_ref[pl.ds(pl.multiple_of(j * TG * rows, TG * rows), TG * rows), b * 256 : (b + 1) * 256] = theld[member]

        def stage11():
            @pl.when(t == chunks + LAGS[6])
            def _():
                for b in range(8):
                    own_ref[:, b * 256 : (b + 1) * 256] = total[b].T

        fns = (stage0, stage1, stage2, stage3, stage4, stage5, stage6, stage7, stage8, stage9, stage10, stage11)
        for q in SEQ:
            fns[q]()
        return carry

    lax.fori_loop(0, chunks + LAGS[10], step, 0)

    def drain(i, carry):
        for stage, ref in enumerate(
            (pool.at[i, pl.ds(0, 7)], cross_out.at[i], partner.at[i, pl.ds(0, 7)], zfar.at[i], zin.at[i],
             yin.at[i])
        ):
            wait_for(ref, ssem.at[stage, i])
        return carry

    lax.fori_loop(0, chunks, drain, 0)

    def tdrain(j, carry):
        for stage, ref in enumerate((tpool.at[j, pl.ds(0, 7)], tcross_out.at[j], tin.at[j, pl.ds(0, 7)])):
            wait_for(ref, ssem.at[6 + stage, j])
        return carry

    lax.fori_loop(0, chunks // TG, tdrain, 0)


def tiles(dosage, freq, plan, chunks, crossing, collective_id):
    rows = 256 // chunks
    bf16 = jnp.bfloat16
    vmem, smem = pltpu.VMEM, pltpu.SMEM
    return pl.pallas_call(
        functools.partial(kernel, chunks, crossing),
        out_shape=(
            jax.ShapeDtypeStruct((256, 2048), jnp.float32),
            jax.ShapeDtypeStruct((256, 2048), bf16),
            jax.ShapeDtypeStruct((8, 128), jnp.int32),
        ),
        in_specs=[
            pl.BlockSpec(memory_space=smem),
            pl.BlockSpec(memory_space=vmem),
            pl.BlockSpec(memory_space=pl.ANY),
        ],
        out_specs=(pl.BlockSpec(memory_space=vmem),) * 3,
        scratch_shapes=[
            vmem((8, 256, 1024), bf16),
            vmem((chunks, HALF + crossing, rows, 1024), bf16),
            vmem((chunks, crossing, rows, 1024), bf16),
            vmem((chunks, HALF, rows, 1024), bf16),
            vmem((chunks, HALF, rows, 1024), bf16),
            vmem((chunks, 8, HALF * rows, 256), bf16),
            vmem((chunks, 2, HALF * rows, 256), bf16),
            vmem((chunks, 2, HALF * rows, 256), bf16),
            vmem((chunks, 4, HALF * rows, 256), bf16),
            vmem((chunks, HALF * rows, 256), bf16),
            vmem((chunks, HALF * rows, 256), bf16),
            vmem((8, 256, 256), jnp.float32),
            vmem((chunks // TG, 8, TG * rows, 256), bf16),
            vmem((chunks // TG, HALF + crossing, TG * rows, 256), bf16),
            vmem((chunks // TG, crossing, TG * rows, 256), bf16),
            vmem((chunks // TG, HALF, TG * rows, 256), bf16),
            vmem((chunks // TG, HALF, TG * rows, 256), bf16),
            vmem((HALF + crossing, rows, 1024), bf16),
            vmem((HALF + crossing, TG * rows, 256), bf16),
            smem((3, 16), jnp.int32),
            smem((3, 16), jnp.int32),
            smem((16,), jnp.int32),
            smem((16,), jnp.int32),
            smem((16,), jnp.int32),
            smem((2, 16), jnp.int32),
            smem((4, 8), jnp.int32),
            pltpu.SemaphoreType.DMA((chunks,)),
            pltpu.SemaphoreType.DMA((9, chunks)),
            pltpu.SemaphoreType.DMA((9, chunks)),
        ],
        compiler_params=pltpu.CompilerParams(
            collective_id=collective_id, has_side_effects=True, vmem_limit_bytes=60 << 20
        ),
        cost_estimate=pl.CostEstimate(flops=2 * 2048 * 2048 * 1024, bytes_accessed=10 << 20, transcendentals=0),
        name=f"tiles{crossing}",
    )(plan, freq, dosage)


def place(colour_ref, own_ref, other_ref, out_ref):
    own, other = own_ref[...], other_ref[...].astype(jnp.float32)
    first = colour_ref[0, 0] == 0
    out_ref[0] = jnp.where(first, own, other)
    out_ref[1] = jnp.where(first, other, own)


def local(dosage, allele_freq, plan):
    dosage = dosage.reshape(8, 256, 1024)
    freq = allele_freq.reshape(1, 1024)
    upper = jnp.arange(2 * HALF, dtype=jnp.int32)[None, :] >= HALF
    crossings = jnp.sum(((plan >= HALF) != upper).astype(jnp.int32))
    few, some, every = (
        functools.partial(tiles, chunks=CHUNKS, crossing=crossing, collective_id=i)
        for i, crossing in enumerate((5, 6, 8))
    )

    def more(*operands):
        return lax.cond(crossings <= 24, some, every, *operands)

    own, other, colour = lax.cond(crossings <= 20, few, more, dosage, freq, plan)
    return pl.pallas_call(
        place,
        out_shape=jax.ShapeDtypeStruct((2, 256, 2048), jnp.float32),
        grid=(BLOCKS,),
        in_specs=[
            pl.BlockSpec(memory_space=pltpu.SMEM),
            pl.BlockSpec((256 // BLOCKS, 2048), lambda i: (i, 0)),
            pl.BlockSpec((256 // BLOCKS, 2048), lambda i: (i, 0)),
        ],
        out_specs=pl.BlockSpec((2, 256 // BLOCKS, 2048), lambda i: (0, i, 0)),
        name="place",
    )(colour, own, other)


def solution(mesh):
    return jax.shard_map(
        local,
        mesh=mesh,
        in_specs=(P("panel", "snp"), P("snp"), P()),
        out_specs=P(None, ("panel", "snp"), None),
        check_vma=False,
    )
```

```python
import functools
import math

import jax
import jax.numpy as jnp
from jax import lax
from jax.experimental import pallas as pl
from jax.experimental.pallas import tpu as pltpu
from jax.sharding import PartitionSpec as P

MESH = pl.DeviceIdType.MESH
CHUNKS = 8
PRE = 0
SEQ = (0, 1, 2, 4, 3, 5, 6, 7, 8, 9, 10, 11)
LAGS = (0, 1, 2, 3, 4, 4, 5, 5, 6, 7, 8)
TG = 1
EARLY = 2
BLOCKS = 2
HALF = 8
ORDER = (1, 7, 3, 5, 2, 6, 4)


def wait_for(ref, sem):
    pltpu.make_async_copy(ref, ref, sem).wait()


def tables(plan_ref, step_ref, low_ref, colour_ref, to_ref, from_ref, rank_ref, n):
    def start(v, carry):
        nxt = plan_ref[1, plan_ref[0, v]]
        step_ref[0, v] = nxt
        low_ref[0, v] = jnp.minimum(v, nxt)
        return carry

    lax.fori_loop(0, n, start, 0)
    for j in range(2):

        def double(v, carry, j=j):
            nxt = step_ref[j, step_ref[j, v]]
            step_ref[j + 1, v] = nxt
            low_ref[j + 1, v] = jnp.minimum(low_ref[j, v], low_ref[j, nxt])
            return carry

        lax.fori_loop(0, n, double, 0)

    def settle(v, carry):
        first, second = plan_ref[0, v], plan_ref[1, v]
        zero = low_ref[2, v] < low_ref[2, first]
        colour_ref[v] = jnp.where(zero, 0, 1)
        from_ref[v] = jnp.where(zero, first, second)
        to_ref[v] = jnp.where(zero, second, first)
        return carry

    lax.fori_loop(0, n, settle, 0)

    def ranks(v, carry):
        a, b = carry
        restart = lax.rem(v, HALF) == 0
        a, b = jnp.where(restart, 0, a), jnp.where(restart, 0, b)
        rank_ref[0, v] = a
        rank_ref[1, v] = b
        mine = lax.div(v, HALF)
        a = a + jnp.where(lax.div(to_ref[v], HALF) != mine, 1, 0)
        b = b + jnp.where(lax.div(from_ref[v], HALF) != mine, 1, 0)
        return a, b

    lax.fori_loop(0, n, ranks, (jnp.int32(0), jnp.int32(0)))


def kernel(
    chunks, crossing, plan_ref, freq_ref, dosage_ref, own_ref, other_ref, mine_ref,
    std, pool, cross_out, arr_out, partner, part, zfar, zsum, zin, yout, yin, total,
    tout, tpool, tcross_out, tarr_out, tin, held, theld,
    step_ref, low_ref, colour_ref, to_ref, from_ref, rank_ref, slot_ref,
    load_sem, ssem, rsem,
):
    rows = 256 // chunks
    panel, snp = lax.axis_index("panel"), lax.axis_index("snp")
    half, me = lax.div(panel, HALF), lax.rem(panel, HALF)
    base = half * HALF
    z, ylo = lax.div(snp, 2), lax.rem(snp, 2)
    turn = lax.rem(me, 2)

    def peer(d):
        return lax.rem(me + d + turn * (HALF - 2 * d), HALF)

    def slab(d):
        return lax.rem(snp + d + turn * (8 - 2 * d), 8)

    def deep(dz):
        return lax.rem(z + dz, 4)

    across = (lax.rem(panel + HALF, 2 * HALF), snp)
    beside = (panel, z * 2 + 1 - ylo)

    def copy(stage, i, src, dst, where):
        pltpu.make_async_remote_copy(
            src_ref=src, dst_ref=dst, send_sem=ssem.at[stage, i], recv_sem=rsem.at[stage, i],
            device_id=where, device_id_type=MESH,
        ).start()

    greeted = [(base + peer(d), snp) for d in range(1, 8)]
    greeted += [(base + peer(d), slab(d)) for d in range(1, 8)]
    greeted += [(panel, deep(dz) * 2 + ylo) for dz in (1, 3)]
    greeted += [across, beside]
    barrier = pltpu.get_barrier_semaphore()
    for where in greeted:
        pl.semaphore_signal(barrier, inc=1, device_id=where, device_id_type=MESH)
    loads = [
        pltpu.make_async_copy(
            dosage_ref.at[:, pl.ds(i * rows, rows)], std.at[:, pl.ds(i * rows, rows)], load_sem.at[i]
        )
        for i in range(chunks)
    ]
    for load in loads:
        load.start()

    freq = freq_ref[...]
    shift = 2.0 * freq
    scale = 1.0 / jnp.sqrt(2.0 * freq * (1.0 - freq))

    def span(i):
        return pl.ds(pl.multiple_of(i * rows, rows), rows)

    def spread(i):
        for d in ORDER:
            copy(0, i, std.at[peer(d), span(i)], pool.at[i, me], (base + peer(d), snp))

    def standardize(i, carry):
        pltpu.make_async_copy(
            dosage_ref.at[:, span(i)], std.at[:, span(i)], load_sem.at[i]
        ).wait()

        def one(l, c):
            value = (std[l, span(i), :].astype(jnp.float32) - shift) * scale
            std[l, span(i), :] = value.astype(jnp.bfloat16)
            return c

        lax.fori_loop(0, 8, one, 0)
        pool[i, me] = std[me, span(i), :]

        return carry

    tables(plan_ref, step_ref, low_ref, colour_ref, to_ref, from_ref, rank_ref, 2 * HALF)
    for kind, (needs, gives) in enumerate(((from_ref, to_ref), (to_ref, from_ref))):

        def slots(j, carry, kind=kind, needs=needs, gives=gives):
            def pick(v, found):
                hit = (rank_ref[kind, base + v] == j) & (lax.div(gives[base + v], HALF) != half)
                return found + jnp.where(hit, v, 0)

            slot_ref[kind, j] = lax.fori_loop(0, HALF, pick, jnp.int32(0))
            source = needs[base + j]
            slot_ref[2 + kind, j] = jnp.where(
                lax.div(source, HALF) == half, lax.rem(source, HALF), HALF + rank_ref[kind, source]
            )
            return carry

        lax.fori_loop(0, HALF, slots, 0)
    lax.fori_loop(0, EARLY, standardize, 0)
    pl.semaphore_wait(barrier, len(greeted))

    for i in range(EARLY):
        spread(i)
    lax.fori_loop(EARLY, chunks, standardize, 0)

    mine_ref[...] = jnp.full((8, 128), colour_ref[panel], jnp.int32)
    origin = lax.rem(to_ref[panel], HALF)
    multiplier = 1.0 / math.sqrt(8192.0)

    def cross(stage, i, buf, keep, out, kind):
        keep[0:HALF] = buf[i, 0:HALF]
        for j in range(crossing):
            out[i, j] = keep[slot_ref[kind, j]]
        copy(stage, i, out.at[i], buf.at[i, pl.ds(HALF, crossing)], across)

    def arrive(stage, i, buf, keep, out, dst, kind):
        keep[...] = buf[i]
        for d in ORDER:
            w = peer(d)
            out[i, w] = keep[slot_ref[2 + kind, w]]
            copy(stage, i, out.at[i, w], dst.at[i, me], (base + w, snp))
        dst[i, me] = keep[slot_ref[2 + kind, me]]

    def step(t, carry):
        def stage(lag, first=0):
            return t - lag, (t >= lag + first) & (t < lag + chunks)

        def stage0():
            i0 = t + PRE

            @pl.when((i0 >= EARLY) & (i0 < chunks))
            def _():
                spread(i0)

        def stage1():
            i1, on = stage(LAGS[1])

            @pl.when(on)
            def _():
                wait_for(pool.at[i1, pl.ds(0, 7)], rsem.at[0, i1])
                cross(1, i1, pool, held, cross_out, 0)

        def stage2():
            i2, on = stage(LAGS[2])

            @pl.when(on)
            def _():
                wait_for(cross_out.at[i2], rsem.at[1, i2])
                arrive(2, i2, pool, held, arr_out, partner, 0)

        def stage3():
            i3, on = stage(LAGS[3])

            @pl.when(on)
            def _():
                wait_for(partner.at[i3, pl.ds(0, 7)], rsem.at[2, i3])
                block = partner[i3].reshape(HALF * rows, 1024)

                def multiply(owner, y):
                    product = lax.dot_general(
                        block, std[owner * 2 + y], (((1,), (1,)), ((), ())), preferred_element_type=jnp.float32
                    )
                    part[i3, owner * 2 + y] = (product * multiplier).astype(jnp.bfloat16)

                def give(stage, owner, y, dst, to):
                    copy(stage, i3, part.at[i3, owner * 2 + y], dst, (panel, to * 2 + ylo))

                after, before, far = deep(1), deep(3), deep(2)
                multiply(far, 0)
                give(3, far, 0, zfar.at[i3, 0], after)
                multiply(far, 1)
                give(3, far, 1, zfar.at[i3, 1], before)
                multiply(after, 1)
                give(4, after, 1, zin.at[i3, 1], after)
                multiply(before, 0)
                give(4, before, 0, zin.at[i3, 0], before)
                multiply(after, 0)
                multiply(before, 1)
                multiply(z, 0)
                multiply(z, 1)

        def stage4():
            i9, on = stage(LAGS[4])

            @pl.when(on)
            def _():
                wait_for(zfar.at[i9], rsem.at[3, i9])
                for y, to in ((0, deep(1)), (1, deep(3))):
                    value = part[i9, to * 2 + y].astype(jnp.float32) + zfar[i9, y].astype(jnp.float32)
                    zsum[i9, y] = value.astype(jnp.bfloat16)
                    copy(4, i9, zsum.at[i9, y], zin.at[i9, 2 + y], (panel, to * 2 + ylo))

        def stage5():
            i4, on = stage(LAGS[5])

            @pl.when(on)
            def _():
                wait_for(zin.at[i4], rsem.at[4, i4])

                def add(y):
                    return (
                        part[i4, z * 2 + y].astype(jnp.float32)
                        + zin[i4, y].astype(jnp.float32)
                        + zin[i4, 2 + y].astype(jnp.float32)
                    )

                yout[i4] = add(1 - ylo).astype(jnp.bfloat16)
                copy(5, i4, yout.at[i4], yin.at[i4], beside)
                total[:, span(i4)] = add(ylo).reshape(HALF, rows, 256)

        def stage6():
            i5, on = stage(LAGS[6])

            @pl.when(on)
            def _():
                wait_for(yin.at[i5], rsem.at[5, i5])
                value = total[:, span(i5)] + yin[i5].astype(jnp.float32).reshape(HALF, rows, 256)
                total[:, span(i5)] = value
                tout[lax.div(i5, TG), :, pl.ds(pl.multiple_of(lax.rem(i5, TG) * rows, rows), rows)] = value.astype(jnp.bfloat16)

        def group(lag):
            u = t - lag
            return lax.div(u, TG), (u >= 0) & (u < chunks) & (lax.rem(u, TG) == 0)

        def stage7():
            j, on = group(LAGS[7])

            @pl.when(on)
            def _():
                for d in ORDER:
                    copy(6, j, tout.at[j, slab(d)], tpool.at[j, me], (base + peer(d), slab(d)))
                tpool[j, me] = tout[j, snp]

        def stage8():
            j, on = group(LAGS[8])

            @pl.when(on)
            def _():
                wait_for(tpool.at[j, pl.ds(0, 7)], rsem.at[6, j])
                cross(7, j, tpool, theld, tcross_out, 1)

        def stage9():
            j, on = group(LAGS[9])

            @pl.when(on)
            def _():
                wait_for(tcross_out.at[j], rsem.at[7, j])
                arrive(8, j, tpool, theld, tarr_out, tin, 1)

        def stage10():
            j, on = group(LAGS[10])

            @pl.when(on)
            def _():
                wait_for(tin.at[j, pl.ds(0, 7)], rsem.at[8, j])
                theld[0:8] = tin[j]
                for b in range(8):
                    member = lax.rem(snp + origin - b + 8, 8)
                    other_ref[pl.ds(pl.multiple_of(j * TG * rows, TG * rows), TG * rows), b * 256 : (b + 1) * 256] = theld[member]

        def stage11():
            @pl.when(t == chunks + LAGS[6])
            def _():
                for b in range(8):
                    own_ref[:, b * 256 : (b + 1) * 256] = total[b].T

        fns = (stage0, stage1, stage2, stage3, stage4, stage5, stage6, stage7, stage8, stage9, stage10, stage11)
        for q in SEQ:
            fns[q]()
        return carry

    lax.fori_loop(0, chunks + LAGS[10], step, 0)

    def drain(i, carry):
        for stage, ref in enumerate(
            (pool.at[i, pl.ds(0, 7)], cross_out.at[i], partner.at[i, pl.ds(0, 7)], zfar.at[i], zin.at[i],
             yin.at[i])
        ):
            wait_for(ref, ssem.at[stage, i])
        return carry

    lax.fori_loop(0, chunks, drain, 0)

    def tdrain(j, carry):
        for stage, ref in enumerate((tpool.at[j, pl.ds(0, 7)], tcross_out.at[j], tin.at[j, pl.ds(0, 7)])):
            wait_for(ref, ssem.at[6 + stage, j])
        return carry

    lax.fori_loop(0, chunks // TG, tdrain, 0)


def tiles(dosage, freq, plan, chunks, crossing, collective_id):
    rows = 256 // chunks
    bf16 = jnp.bfloat16
    vmem, smem = pltpu.VMEM, pltpu.SMEM
    return pl.pallas_call(
        functools.partial(kernel, chunks, crossing),
        out_shape=(
            jax.ShapeDtypeStruct((256, 2048), jnp.float32),
            jax.ShapeDtypeStruct((256, 2048), bf16),
            jax.ShapeDtypeStruct((8, 128), jnp.int32),
        ),
        in_specs=[
            pl.BlockSpec(memory_space=smem),
            pl.BlockSpec(memory_space=vmem),
            pl.BlockSpec(memory_space=pl.ANY),
        ],
        out_specs=(pl.BlockSpec(memory_space=vmem),) * 3,
        scratch_shapes=[
            vmem((8, 256, 1024), bf16),
            vmem((chunks, HALF + crossing, rows, 1024), bf16),
            vmem((chunks, crossing, rows, 1024), bf16),
            vmem((chunks, HALF, rows, 1024), bf16),
            vmem((chunks, HALF, rows, 1024), bf16),
            vmem((chunks, 8, HALF * rows, 256), bf16),
            vmem((chunks, 2, HALF * rows, 256), bf16),
            vmem((chunks, 2, HALF * rows, 256), bf16),
            vmem((chunks, 4, HALF * rows, 256), bf16),
            vmem((chunks, HALF * rows, 256), bf16),
            vmem((chunks, HALF * rows, 256), bf16),
            vmem((8, 256, 256), jnp.float32),
            vmem((chunks // TG, 8, TG * rows, 256), bf16),
            vmem((chunks // TG, HALF + crossing, TG * rows, 256), bf16),
            vmem((chunks // TG, crossing, TG * rows, 256), bf16),
            vmem((chunks // TG, HALF, TG * rows, 256), bf16),
            vmem((chunks // TG, HALF, TG * rows, 256), bf16),
            vmem((HALF + crossing, rows, 1024), bf16),
            vmem((HALF + crossing, TG * rows, 256), bf16),
            smem((3, 16), jnp.int32),
            smem((3, 16), jnp.int32),
            smem((16,), jnp.int32),
            smem((16,), jnp.int32),
            smem((16,), jnp.int32),
            smem((2, 16), jnp.int32),
            smem((4, 8), jnp.int32),
            pltpu.SemaphoreType.DMA((chunks,)),
            pltpu.SemaphoreType.DMA((9, chunks)),
            pltpu.SemaphoreType.DMA((9, chunks)),
        ],
        compiler_params=pltpu.CompilerParams(
            collective_id=collective_id, has_side_effects=True, vmem_limit_bytes=60 << 20
        ),
        cost_estimate=pl.CostEstimate(flops=2 * 2048 * 2048 * 1024, bytes_accessed=10 << 20, transcendentals=0),
        name=f"tiles{crossing}",
    )(plan, freq, dosage)


def place(colour_ref, own_ref, other_ref, out_ref):
    own, other = own_ref[...], other_ref[...].astype(jnp.float32)
    first = colour_ref[0, 0] == 0
    out_ref[0] = jnp.where(first, own, other)
    out_ref[1] = jnp.where(first, other, own)


def local(dosage, allele_freq, plan):
    dosage = dosage.reshape(8, 256, 1024)
    freq = allele_freq.reshape(1, 1024)
    upper = jnp.arange(2 * HALF, dtype=jnp.int32)[None, :] >= HALF
    crossings = jnp.sum(((plan >= HALF) != upper).astype(jnp.int32))
    few, some, every = (
        functools.partial(tiles, chunks=CHUNKS, crossing=crossing, collective_id=i)
        for i, crossing in enumerate((5, 6, 8))
    )

    def more(*operands):
        return lax.cond(crossings <= 24, some, every, *operands)

    own, other, colour = lax.cond(crossings <= 20, few, more, dosage, freq, plan)
    return pl.pallas_call(
        place,
        out_shape=jax.ShapeDtypeStruct((2, 256, 2048), jnp.float32),
        grid=(BLOCKS,),
        in_specs=[
            pl.BlockSpec(memory_space=pltpu.SMEM),
            pl.BlockSpec((256 // BLOCKS, 2048), lambda i: (i, 0)),
            pl.BlockSpec((256 // BLOCKS, 2048), lambda i: (i, 0)),
        ],
        out_specs=pl.BlockSpec((2, 256 // BLOCKS, 2048), lambda i: (0, i, 0)),
        name="place",
    )(colour, own, other)


def solution(mesh):
    return jax.shard_map(
        local,
        mesh=mesh,
        in_specs=(P("panel", "snp"), P("snp"), P()),
        out_specs=P(None, ("panel", "snp"), None),
        check_vma=False,
    )
```

```python
import functools
import math

import jax
import jax.numpy as jnp
from jax import lax
from jax.experimental import pallas as pl
from jax.experimental.pallas import tpu as pltpu
from jax.sharding import PartitionSpec as P

MESH = pl.DeviceIdType.MESH
CHUNKS = 8
PRE = 0
SEQ = (0, 2, 1, 4, 3, 5, 6, 7, 8, 9, 10, 11)
LAGS = (0, 1, 2, 3, 4, 4, 5, 5, 6, 7, 8)
TG = 1
EARLY = 2
BLOCKS = 2
HALF = 8
ORDER = (1, 7, 3, 5, 2, 6, 4)


def wait_for(ref, sem):
    pltpu.make_async_copy(ref, ref, sem).wait()


def tables(plan_ref, step_ref, low_ref, colour_ref, to_ref, from_ref, rank_ref, n):
    def start(v, carry):
        nxt = plan_ref[1, plan_ref[0, v]]
        step_ref[0, v] = nxt
        low_ref[0, v] = jnp.minimum(v, nxt)
        return carry

    lax.fori_loop(0, n, start, 0)
    for j in range(2):

        def double(v, carry, j=j):
            nxt = step_ref[j, step_ref[j, v]]
            step_ref[j + 1, v] = nxt
            low_ref[j + 1, v] = jnp.minimum(low_ref[j, v], low_ref[j, nxt])
            return carry

        lax.fori_loop(0, n, double, 0)

    def settle(v, carry):
        first, second = plan_ref[0, v], plan_ref[1, v]
        zero = low_ref[2, v] < low_ref[2, first]
        colour_ref[v] = jnp.where(zero, 0, 1)
        from_ref[v] = jnp.where(zero, first, second)
        to_ref[v] = jnp.where(zero, second, first)
        return carry

    lax.fori_loop(0, n, settle, 0)

    def ranks(v, carry):
        a, b = carry
        restart = lax.rem(v, HALF) == 0
        a, b = jnp.where(restart, 0, a), jnp.where(restart, 0, b)
        rank_ref[0, v] = a
        rank_ref[1, v] = b
        mine = lax.div(v, HALF)
        a = a + jnp.where(lax.div(to_ref[v], HALF) != mine, 1, 0)
        b = b + jnp.where(lax.div(from_ref[v], HALF) != mine, 1, 0)
        return a, b

    lax.fori_loop(0, n, ranks, (jnp.int32(0), jnp.int32(0)))


def kernel(
    chunks, crossing, plan_ref, freq_ref, dosage_ref, own_ref, other_ref, mine_ref,
    std, pool, cross_out, arr_out, partner, part, zfar, zsum, zin, yout, yin, total,
    tout, tpool, tcross_out, tarr_out, tin, held, theld,
    step_ref, low_ref, colour_ref, to_ref, from_ref, rank_ref, slot_ref,
    load_sem, ssem, rsem,
):
    rows = 256 // chunks
    panel, snp = lax.axis_index("panel"), lax.axis_index("snp")
    half, me = lax.div(panel, HALF), lax.rem(panel, HALF)
    base = half * HALF
    z, ylo = lax.div(snp, 2), lax.rem(snp, 2)
    turn = lax.rem(me, 2)

    def peer(d):
        return lax.rem(me + d + turn * (HALF - 2 * d), HALF)

    def slab(d):
        return lax.rem(snp + d + turn * (8 - 2 * d), 8)

    def deep(dz):
        return lax.rem(z + dz, 4)

    across = (lax.rem(panel + HALF, 2 * HALF), snp)
    beside = (panel, z * 2 + 1 - ylo)

    def copy(stage, i, src, dst, where):
        pltpu.make_async_remote_copy(
            src_ref=src, dst_ref=dst, send_sem=ssem.at[stage, i], recv_sem=rsem.at[stage, i],
            device_id=where, device_id_type=MESH,
        ).start()

    greeted = [(base + peer(d), snp) for d in range(1, 8)]
    greeted += [(base + peer(d), slab(d)) for d in range(1, 8)]
    greeted += [(panel, deep(dz) * 2 + ylo) for dz in (1, 3)]
    greeted += [across, beside]
    barrier = pltpu.get_barrier_semaphore()
    for where in greeted:
        pl.semaphore_signal(barrier, inc=1, device_id=where, device_id_type=MESH)
    loads = [
        pltpu.make_async_copy(
            dosage_ref.at[:, pl.ds(i * rows, rows)], std.at[:, pl.ds(i * rows, rows)], load_sem.at[i]
        )
        for i in range(chunks)
    ]
    for load in loads:
        load.start()

    freq = freq_ref[...]
    shift = 2.0 * freq
    scale = 1.0 / jnp.sqrt(2.0 * freq * (1.0 - freq))

    def span(i):
        return pl.ds(pl.multiple_of(i * rows, rows), rows)

    def spread(i):
        for d in ORDER:
            copy(0, i, std.at[peer(d), span(i)], pool.at[i, me], (base + peer(d), snp))

    def standardize(i, carry):
        pltpu.make_async_copy(
            dosage_ref.at[:, span(i)], std.at[:, span(i)], load_sem.at[i]
        ).wait()

        def one(l, c):
            value = (std[l, span(i), :].astype(jnp.float32) - shift) * scale
            std[l, span(i), :] = value.astype(jnp.bfloat16)
            return c

        lax.fori_loop(0, 8, one, 0)
        pool[i, me] = std[me, span(i), :]

        return carry

    tables(plan_ref, step_ref, low_ref, colour_ref, to_ref, from_ref, rank_ref, 2 * HALF)
    for kind, (needs, gives) in enumerate(((from_ref, to_ref), (to_ref, from_ref))):

        def slots(j, carry, kind=kind, needs=needs, gives=gives):
            def pick(v, found):
                hit = (rank_ref[kind, base + v] == j) & (lax.div(gives[base + v], HALF) != half)
                return found + jnp.where(hit, v, 0)

            slot_ref[kind, j] = lax.fori_loop(0, HALF, pick, jnp.int32(0))
            source = needs[base + j]
            slot_ref[2 + kind, j] = jnp.where(
                lax.div(source, HALF) == half, lax.rem(source, HALF), HALF + rank_ref[kind, source]
            )
            return carry

        lax.fori_loop(0, HALF, slots, 0)
    lax.fori_loop(0, EARLY, standardize, 0)
    pl.semaphore_wait(barrier, len(greeted))

    for i in range(EARLY):
        spread(i)
    lax.fori_loop(EARLY, chunks, standardize, 0)

    mine_ref[...] = jnp.full((8, 128), colour_ref[panel], jnp.int32)
    origin = lax.rem(to_ref[panel], HALF)
    multiplier = 1.0 / math.sqrt(8192.0)

    def cross(stage, i, buf, keep, out, kind):
        keep[0:HALF] = buf[i, 0:HALF]
        for j in range(crossing):
            out[i, j] = keep[slot_ref[kind, j]]
        copy(stage, i, out.at[i], buf.at[i, pl.ds(HALF, crossing)], across)

    def arrive(stage, i, buf, keep, out, dst, kind):
        keep[...] = buf[i]
        for d in ORDER:
            w = peer(d)
            out[i, w] = keep[slot_ref[2 + kind, w]]
            copy(stage, i, out.at[i, w], dst.at[i, me], (base + w, snp))
        dst[i, me] = keep[slot_ref[2 + kind, me]]

    def step(t, carry):
        def stage(lag, first=0):
            return t - lag, (t >= lag + first) & (t < lag + chunks)

        def stage0():
            i0 = t + PRE

            @pl.when((i0 >= EARLY) & (i0 < chunks))
            def _():
                spread(i0)

        def stage1():
            i1, on = stage(LAGS[1])

            @pl.when(on)
            def _():
                wait_for(pool.at[i1, pl.ds(0, 7)], rsem.at[0, i1])
                cross(1, i1, pool, held, cross_out, 0)

        def stage2():
            i2, on = stage(LAGS[2])

            @pl.when(on)
            def _():
                wait_for(cross_out.at[i2], rsem.at[1, i2])
                arrive(2, i2, pool, held, arr_out, partner, 0)

        def stage3():
            i3, on = stage(LAGS[3])

            @pl.when(on)
            def _():
                wait_for(partner.at[i3, pl.ds(0, 7)], rsem.at[2, i3])
                block = partner[i3].reshape(HALF * rows, 1024)

                def multiply(owner, y):
                    product = lax.dot_general(
                        block, std[owner * 2 + y], (((1,), (1,)), ((), ())), preferred_element_type=jnp.float32
                    )
                    part[i3, owner * 2 + y] = (product * multiplier).astype(jnp.bfloat16)

                def give(stage, owner, y, dst, to):
                    copy(stage, i3, part.at[i3, owner * 2 + y], dst, (panel, to * 2 + ylo))

                after, before, far = deep(1), deep(3), deep(2)
                multiply(far, 0)
                give(3, far, 0, zfar.at[i3, 0], after)
                multiply(far, 1)
                give(3, far, 1, zfar.at[i3, 1], before)
                multiply(after, 1)
                give(4, after, 1, zin.at[i3, 1], after)
                multiply(before, 0)
                give(4, before, 0, zin.at[i3, 0], before)
                multiply(after, 0)
                multiply(before, 1)
                multiply(z, 0)
                multiply(z, 1)

        def stage4():
            i9, on = stage(LAGS[4])

            @pl.when(on)
            def _():
                wait_for(zfar.at[i9], rsem.at[3, i9])
                for y, to in ((0, deep(1)), (1, deep(3))):
                    value = part[i9, to * 2 + y].astype(jnp.float32) + zfar[i9, y].astype(jnp.float32)
                    zsum[i9, y] = value.astype(jnp.bfloat16)
                    copy(4, i9, zsum.at[i9, y], zin.at[i9, 2 + y], (panel, to * 2 + ylo))

        def stage5():
            i4, on = stage(LAGS[5])

            @pl.when(on)
            def _():
                wait_for(zin.at[i4], rsem.at[4, i4])

                def add(y):
                    return (
                        part[i4, z * 2 + y].astype(jnp.float32)
                        + zin[i4, y].astype(jnp.float32)
                        + zin[i4, 2 + y].astype(jnp.float32)
                    )

                yout[i4] = add(1 - ylo).astype(jnp.bfloat16)
                copy(5, i4, yout.at[i4], yin.at[i4], beside)
                total[:, span(i4)] = add(ylo).reshape(HALF, rows, 256)

        def stage6():
            i5, on = stage(LAGS[6])

            @pl.when(on)
            def _():
                wait_for(yin.at[i5], rsem.at[5, i5])
                value = total[:, span(i5)] + yin[i5].astype(jnp.float32).reshape(HALF, rows, 256)
                total[:, span(i5)] = value
                tout[lax.div(i5, TG), :, pl.ds(pl.multiple_of(lax.rem(i5, TG) * rows, rows), rows)] = value.astype(jnp.bfloat16)

        def group(lag):
            u = t - lag
            return lax.div(u, TG), (u >= 0) & (u < chunks) & (lax.rem(u, TG) == 0)

        def stage7():
            j, on = group(LAGS[7])

            @pl.when(on)
            def _():
                for d in ORDER:
                    copy(6, j, tout.at[j, slab(d)], tpool.at[j, me], (base + peer(d), slab(d)))
                tpool[j, me] = tout[j, snp]

        def stage8():
            j, on = group(LAGS[8])

            @pl.when(on)
            def _():
                wait_for(tpool.at[j, pl.ds(0, 7)], rsem.at[6, j])
                cross(7, j, tpool, theld, tcross_out, 1)

        def stage9():
            j, on = group(LAGS[9])

            @pl.when(on)
            def _():
                wait_for(tcross_out.at[j], rsem.at[7, j])
                arrive(8, j, tpool, theld, tarr_out, tin, 1)

        def stage10():
            j, on = group(LAGS[10])

            @pl.when(on)
            def _():
                wait_for(tin.at[j, pl.ds(0, 7)], rsem.at[8, j])
                theld[0:8] = tin[j]
                for b in range(8):
                    member = lax.rem(snp + origin - b + 8, 8)
                    other_ref[pl.ds(pl.multiple_of(j * TG * rows, TG * rows), TG * rows), b * 256 : (b + 1) * 256] = theld[member]

        def stage11():
            @pl.when(t == chunks + LAGS[6])
            def _():
                for b in range(8):
                    own_ref[:, b * 256 : (b + 1) * 256] = total[b].T

        fns = (stage0, stage1, stage2, stage3, stage4, stage5, stage6, stage7, stage8, stage9, stage10, stage11)
        for q in SEQ:
            fns[q]()
        return carry

    lax.fori_loop(0, chunks + LAGS[10], step, 0)

    def drain(i, carry):
        for stage, ref in enumerate(
            (pool.at[i, pl.ds(0, 7)], cross_out.at[i], partner.at[i, pl.ds(0, 7)], zfar.at[i], zin.at[i],
             yin.at[i])
        ):
            wait_for(ref, ssem.at[stage, i])
        return carry

    lax.fori_loop(0, chunks, drain, 0)

    def tdrain(j, carry):
        for stage, ref in enumerate((tpool.at[j, pl.ds(0, 7)], tcross_out.at[j], tin.at[j, pl.ds(0, 7)])):
            wait_for(ref, ssem.at[6 + stage, j])
        return carry

    lax.fori_loop(0, chunks // TG, tdrain, 0)


def tiles(dosage, freq, plan, chunks, crossing, collective_id):
    rows = 256 // chunks
    bf16 = jnp.bfloat16
    vmem, smem = pltpu.VMEM, pltpu.SMEM
    return pl.pallas_call(
        functools.partial(kernel, chunks, crossing),
        out_shape=(
            jax.ShapeDtypeStruct((256, 2048), jnp.float32),
            jax.ShapeDtypeStruct((256, 2048), bf16),
            jax.ShapeDtypeStruct((8, 128), jnp.int32),
        ),
        in_specs=[
            pl.BlockSpec(memory_space=smem),
            pl.BlockSpec(memory_space=vmem),
            pl.BlockSpec(memory_space=pl.ANY),
        ],
        out_specs=(pl.BlockSpec(memory_space=vmem),) * 3,
        scratch_shapes=[
            vmem((8, 256, 1024), bf16),
            vmem((chunks, HALF + crossing, rows, 1024), bf16),
            vmem((chunks, crossing, rows, 1024), bf16),
            vmem((chunks, HALF, rows, 1024), bf16),
            vmem((chunks, HALF, rows, 1024), bf16),
            vmem((chunks, 8, HALF * rows, 256), bf16),
            vmem((chunks, 2, HALF * rows, 256), bf16),
            vmem((chunks, 2, HALF * rows, 256), bf16),
            vmem((chunks, 4, HALF * rows, 256), bf16),
            vmem((chunks, HALF * rows, 256), bf16),
            vmem((chunks, HALF * rows, 256), bf16),
            vmem((8, 256, 256), jnp.float32),
            vmem((chunks // TG, 8, TG * rows, 256), bf16),
            vmem((chunks // TG, HALF + crossing, TG * rows, 256), bf16),
            vmem((chunks // TG, crossing, TG * rows, 256), bf16),
            vmem((chunks // TG, HALF, TG * rows, 256), bf16),
            vmem((chunks // TG, HALF, TG * rows, 256), bf16),
            vmem((HALF + crossing, rows, 1024), bf16),
            vmem((HALF + crossing, TG * rows, 256), bf16),
            smem((3, 16), jnp.int32),
            smem((3, 16), jnp.int32),
            smem((16,), jnp.int32),
            smem((16,), jnp.int32),
            smem((16,), jnp.int32),
            smem((2, 16), jnp.int32),
            smem((4, 8), jnp.int32),
            pltpu.SemaphoreType.DMA((chunks,)),
            pltpu.SemaphoreType.DMA((9, chunks)),
            pltpu.SemaphoreType.DMA((9, chunks)),
        ],
        compiler_params=pltpu.CompilerParams(
            collective_id=collective_id, has_side_effects=True, vmem_limit_bytes=60 << 20
        ),
        cost_estimate=pl.CostEstimate(flops=2 * 2048 * 2048 * 1024, bytes_accessed=10 << 20, transcendentals=0),
        name=f"tiles{crossing}",
    )(plan, freq, dosage)


def place(colour_ref, own_ref, other_ref, out_ref):
    own, other = own_ref[...], other_ref[...].astype(jnp.float32)
    first = colour_ref[0, 0] == 0
    out_ref[0] = jnp.where(first, own, other)
    out_ref[1] = jnp.where(first, other, own)


def local(dosage, allele_freq, plan):
    dosage = dosage.reshape(8, 256, 1024)
    freq = allele_freq.reshape(1, 1024)
    upper = jnp.arange(2 * HALF, dtype=jnp.int32)[None, :] >= HALF
    crossings = jnp.sum(((plan >= HALF) != upper).astype(jnp.int32))
    few, some, every = (
        functools.partial(tiles, chunks=CHUNKS, crossing=crossing, collective_id=i)
        for i, crossing in enumerate((5, 6, 8))
    )

    def more(*operands):
        return lax.cond(crossings <= 24, some, every, *operands)

    own, other, colour = lax.cond(crossings <= 20, few, more, dosage, freq, plan)
    return pl.pallas_call(
        place,
        out_shape=jax.ShapeDtypeStruct((2, 256, 2048), jnp.float32),
        grid=(BLOCKS,),
        in_specs=[
            pl.BlockSpec(memory_space=pltpu.SMEM),
            pl.BlockSpec((256 // BLOCKS, 2048), lambda i: (i, 0)),
            pl.BlockSpec((256 // BLOCKS, 2048), lambda i: (i, 0)),
        ],
        out_specs=pl.BlockSpec((2, 256 // BLOCKS, 2048), lambda i: (0, i, 0)),
        name="place",
    )(colour, own, other)


def solution(mesh):
    return jax.shard_map(
        local,
        mesh=mesh,
        in_specs=(P("panel", "snp"), P("snp"), P()),
        out_specs=P(None, ("panel", "snp"), None),
        check_vma=False,
    )
```
